256 devices in a mesh: shot: 64 (over y, z_hi, x), gz: 4 (over z_lo, core).
Axes of the slice: x: 4, y: 4, z: 8 (z_hi: 4, z_lo: 2; z = z_hi * 2 + z_lo), core: 2. Of those that a mesh axis runs over, the one named last changes fastest.
Arguments:
- squared_courant: float32 [128, 512, 128], P('gz', 'shot'), may hold values from 0.05 to 0.19
- window_offset: int32 [64], P('shot'), may hold values from -2 to 2, as said below
- field_last: float32 [64, 128, 64, 128], P('shot', 'gz'), may hold values from -4 to 4
- field_after: float32 [64, 128, 64, 128], P('shot', 'gz'), may hold values from -4 to 4
- adjoint_last: float32 [64, 128, 64, 128], P('shot', 'gz'), may hold values from -4 to 4
- adjoint_after: float32 [64, 128, 64, 128], P('shot', 'gz'), may hold values from -4 to 4
- source_place: int32 [64, 3], P('shot'), may hold values from 0 to 127, as said below
- source_wavelet: float32 [64, 4], P('shot'), may hold values from -12 to 12
- receiver_place: int32 [64, 3, 128], P('shot'), may hold values from 0 to 127, as said below
- receiver_trace: float32 [64, 4, 128], P('shot'), may hold values from -6 to 6
Outputs:
- field_early: float32 [64, 128, 64, 128], P('shot', 'gz')
- adjoint_early: float32 [64, 128, 64, 128], P('shot', 'gz')
- model_gradient: float32 [128, 512, 128], P('gz', 'shot')
The draws below stay inside these ranges and needn't reach their ends.
Inputs may be any that keep to these rules, and one draw needn't show every extreme that they name: `window_offset`: offsets of -2 and 2 both occur. `source_place`: column 0 is below 128, column 1 below 64, column 2 below 128. `receiver_place`: row 0 is below 128, row 1 below 64, row 2 below 128; receivers may share cells.
All inputs are finite; a program needn't handle non-finite values.
Results may differ from the reference program's by a relative error of at most 0.00002.
Values sent between devices are 32-bit elements; how exact they have to be, the bound alone decides.
A program may use at most 128 MiB of HBM per device.

```python
import math
import jax
import jax.numpy as jnp
from jax import lax

BX = 8
SPREAD = 2
YW = 128
STEPS = 4
NREC = 128
SHOTS = 64
NZ = 128
WX = 64
NXG = 512


def draw_window_offset(key, part):
    key = jax.random.fold_in(key, 11)
    first, second = jax.random.split(key)
    offsets = jax.random.randint(first, (SHOTS,), -SPREAD, SPREAD + 1)
    order = jax.random.permutation(second, SHOTS)
    offsets = offsets.at[order[0]].set(-SPREAD).at[order[1]].set(SPREAD)
    return offsets.astype(jnp.int32)


def draw_source_place(key, part):
    key = jax.random.fold_in(key, 12)
    keys = jax.random.split(key, 4)
    depth = jax.random.randint(keys[0], (SHOTS,), 0, NZ)
    across = jax.random.randint(keys[1], (SHOTS,), 0, WX)
    along = jax.random.randint(keys[2], (SHOTS,), 0, YW)
    order = jax.random.permutation(keys[3], SHOTS)
    depth = depth.at[order[0]].set(NZ - 1).at[order[1]].set(0)
    across = across.at[order[0]].set(WX - 1).at[order[1]].set(0)
    along = along.at[order[0]].set(YW - 1).at[order[1]].set(0)
    return jnp.stack([depth, across, along], axis=1).astype(jnp.int32)


def draw_receiver_place(key, part):
    key = jax.random.fold_in(key, 13)
    keys = jax.random.split(key, 4)
    depth = jax.random.randint(keys[0], (SHOTS, NREC), 0, NZ)
    across = jax.random.randint(keys[1], (SHOTS, NREC), 0, WX)
    along = jax.random.randint(keys[2], (SHOTS, NREC), 0, YW)
    chosen = jax.random.randint(keys[3], (), 0, SHOTS)
    depth = depth.at[chosen, 0].set(NZ - 1).at[chosen, 1].set(0)
    across = across.at[chosen, 0].set(WX - 1).at[chosen, 1].set(0)
    along = along.at[chosen, 0].set(YW - 1).at[chosen, 1].set(0)
    return jnp.stack([depth, across, along], axis=1).astype(jnp.int32)


def block_levels(own_key, dims, shards, least, high):
    factor_of = 1.0
    for axis_at, parts in shards:
        draws = jax.random.uniform(jax.random.fold_in(jax.random.fold_in(own_key, 6), axis_at), (parts,), jnp.float32, least / len(shards), high / len(shards))
        factor_of = factor_of * jnp.repeat(jnp.exp(draws), dims[axis_at] // parts).reshape((-1,) + (1,) * (len(dims) - 1 - axis_at))
    return factor_of


def noise(stream_key, extent, scale, most, pieces=(), kind=jnp.bfloat16):
    entries = scale * jax.random.normal(stream_key, extent, jnp.float32)
    if pieces:
        entries = entries * block_levels(stream_key, extent, pieces, -0.22, 0.18)
    return jnp.clip(entries, -most, most).astype(kind)


def setup_inputs(seed: int = 0) -> dict:
    key_of = jax.random.split(jax.random.key(seed), 11)
    return {
        "squared_courant": jnp.clip(0.05 + 0.14 * jax.random.uniform(key_of[0], (NZ, NXG, YW), jnp.float32) ** block_levels(key_of[0], (NZ, NXG, YW), ((0, 4), (1, 64)), -0.2, 0.2), 0.05, 0.19),
        "window_offset": draw_window_offset(jax.random.fold_in(key_of[10], 71), 0),
        "field_last": noise(key_of[2], (SHOTS, NZ, WX, YW), 0.3, 4.0, ((0, 64), (1, 4)), jnp.float32),
        "field_after": noise(key_of[3], (SHOTS, NZ, WX, YW), 0.3, 4.0, ((0, 64), (1, 4)), jnp.float32),
        "adjoint_last": noise(key_of[4], (SHOTS, NZ, WX, YW), 0.3, 4.0, ((0, 64), (1, 4)), jnp.float32),
        "adjoint_after": noise(key_of[5], (SHOTS, NZ, WX, YW), 0.3, 4.0, ((0, 64), (1, 4)), jnp.float32),
        "source_place": draw_source_place(jax.random.fold_in(key_of[10], 71), 0),
        "source_wavelet": noise(key_of[7], (SHOTS, STEPS), 3.0, 12.0, ((0, 64),), jnp.float32),
        "receiver_place": draw_receiver_place(jax.random.fold_in(key_of[10], 71), 0),
        "receiver_trace": noise(key_of[9], (SHOTS, STEPS, NREC), 1.0, 6.0, ((0, 64),), jnp.float32),
    }


stencil_weights = (-205.0 / 72.0, 8.0 / 5.0, -1.0 / 5.0, 8.0 / 315.0, -1.0 / 560.0)


def apply_stencil(padded):
    depth = padded.shape[0] - 8
    width = padded.shape[1] - 8
    across = padded.shape[2] - 8
    result = (3.0 * stencil_weights[0]) * padded[4:4 + depth, 4:4 + width, 4:4 + across]
    for k in range(1, 5):
        result = result + stencil_weights[k] * (
            padded[4 + k:4 + k + depth, 4:4 + width, 4:4 + across]
            + padded[4 - k:4 - k + depth, 4:4 + width, 4:4 + across]
            + padded[4:4 + depth, 4 + k:4 + k + width, 4:4 + across]
            + padded[4:4 + depth, 4 - k:4 - k + width, 4:4 + across]
            + padded[4:4 + depth, 4:4 + width, 4 + k:4 + k + across]
            + padded[4:4 + depth, 4:4 + width, 4 - k:4 - k + across])
    return result


def laplace(field):
    return apply_stencil(jnp.pad(field, 4))


def reference(squared_courant, window_offset, field_last, field_after, adjoint_last, adjoint_after,
              source_place, source_wavelet, receiver_place, receiver_trace):
    tapering = jnp.sin(math.pi * (jnp.arange(WX, dtype=jnp.float32) + 0.5) / WX) ** 2

    def one_shot(gradient, inputs):
        shot_index, offset, field_now, field_next, adjoint_now, adjoint_next, places, wavelet, receivers, traces = inputs
        window_start = (shot_index + offset) * BX
        window_model = jnp.roll(squared_courant, -window_start, axis=1)[:, :WX]
        imaging = jnp.zeros((NZ, WX, YW), jnp.float32)
        for step in range(STEPS):
            lap_field = laplace(field_now)
            lap_adjoint = laplace(adjoint_now)
            imaging = imaging + adjoint_now * lap_field
            source = jnp.zeros((NZ, WX, YW), jnp.float32).at[places[0], places[1], places[2]].add(wavelet[step])
            injected = jnp.zeros((NZ, WX, YW), jnp.float32).at[receivers[0], receivers[1], receivers[2]].add(traces[step])
            field_new = 2.0 * field_now - field_next + window_model * lap_field + source
            adjoint_new = 2.0 * adjoint_now - adjoint_next + window_model * lap_adjoint + injected
            field_next, field_now = field_now, field_new
            adjoint_next, adjoint_now = adjoint_now, adjoint_new
        weighted = tapering[None, :, None] * imaging
        placed = jnp.zeros((NZ, NXG, YW), jnp.float32).at[:, :WX].set(weighted)
        gradient = gradient + jnp.roll(placed, window_start, axis=1)
        return gradient, (field_now, adjoint_now)

    shot_ids = jnp.arange(SHOTS, dtype=jnp.int32)
    gradient, outputs = lax.scan(
        one_shot, jnp.zeros((NZ, NXG, YW), jnp.float32),
        (shot_ids, window_offset, field_last, field_after, adjoint_last, adjoint_after,
         source_place, source_wavelet, receiver_place, receiver_trace))
    return outputs[0], outputs[1], gradient
```

```python
import functools
import math

import jax
import jax.numpy as jnp
import numpy as np
from jax import lax
from jax.experimental import pallas as pl
from jax.experimental.pallas import tpu as pltpu
from jax.sharding import PartitionSpec as P

WB = 8
SPREAD = 2
STEPS = 4
SPAN = WB + 2 * SPREAD
HALO = 4
CHUNK = 4
SCALE = 5040.0
CENTRE = -3.0 * 14350.0
SIDE = (8064.0, -1008.0, 128.0, -9.0)
MESH = pl.DeviceIdType.MESH


def banded(rows, cols, period):
    i = lax.broadcasted_iota(jnp.int32, (rows, cols), 0)
    j = lax.broadcasted_iota(jnp.int32, (rows, cols), 1)
    gap = jnp.abs(lax.rem(i, period) - lax.rem(j, period))
    band = jnp.zeros((rows, cols), jnp.float32)
    for k in range(1, 5):
        band = jnp.where(gap == k, SIDE[k - 1], band)
    return band.astype(jnp.bfloat16)


def in_two(values):
    high = values.astype(jnp.bfloat16)
    low = (values - high.astype(jnp.float32)).astype(jnp.bfloat16)
    return high, low


def kernel(
    offset_ref,
    spot_ref,
    wavelet_ref,
    receivers_ref,
    traces_ref,
    taper_ref,
    courant_ref,
    field_last,
    field_after,
    adjoint_last,
    adjoint_after,
    field_out,
    adjoint_out,
    gradient_out,
    fields,
    pieces,
    laps,
    model,
    imaging,
    shown,
    outgoing,
    arriving,
    gradient,
    hits,
    amounts,
    load_sem,
    halo_send,
    halo_recv,
    piece_send,
    piece_recv,
    back_send,
    back_recv,
):
    shot = lax.axis_index("shot")
    slab = lax.axis_index("gz")
    shots = lax.axis_size("shot")
    slabs = lax.axis_size("gz")
    depth, width, across = field_last.shape
    chunks = depth // CHUNK
    has = (slab > 0, slab < slabs - 1)
    beside = (jnp.maximum(slab - 1, 0), jnp.minimum(slab + 1, slabs - 1))

    def partner(k):
        return lax.rem(shot + k + shots, shots)

    loads = []
    for i, (buffer, which, source) in enumerate(
        ((0, 0, field_last), (0, 1, adjoint_last), (1, 0, field_after), (1, 1, adjoint_after))
    ):
        loads.append(pltpu.make_async_copy(source, fields.at[buffer, which, pl.ds(HALO, depth)], load_sem.at[i]))
    loads.append(pltpu.make_async_copy(courant_ref, pieces.at[SPREAD], load_sem.at[4]))
    for copy in loads:
        copy.start()

    blank = jnp.zeros((HALO, width, across), jnp.float32)
    for side, place in ((0, 0), (1, HALO + depth)):

        @pl.when(jnp.logical_not(has[side]))
        def _():
            for buffer in range(2):
                for which in range(2):
                    fields[buffer, which, pl.ds(place, HALO)] = blank

    barrier = pltpu.get_barrier_semaphore()
    for k in range(-(SPAN - SPREAD - 1), SPAN - SPREAD):
        if k != 0:
            pl.semaphore_signal(barrier, inc=1, device_id={"shot": partner(k)}, device_id_type=MESH)
    for side in range(2):

        @pl.when(has[side])
        def _():
            pl.semaphore_signal(barrier, inc=1, device_id={"gz": beside[side]}, device_id_type=MESH)

    beside_count = jnp.where(has[0], 1, 0) + jnp.where(has[1], 1, 0)
    pl.semaphore_wait(barrier, 2 * (SPAN - SPREAD - 1) + beside_count)

    def halo(turn, which, side):
        place = HALO if side == 0 else depth
        landing = HALO + depth if side == 0 else 0
        if turn == 0:
            source = (field_last, adjoint_last)[which].at[pl.ds(place - HALO, HALO)]
        else:
            source = fields.at[turn % 2, which, pl.ds(place, HALO)]
        return pltpu.make_async_remote_copy(
            src_ref=source,
            dst_ref=fields.at[turn % 2, which, pl.ds(landing, HALO)],
            send_sem=halo_send.at[turn, which, side],
            recv_sem=halo_recv.at[turn, which, side],
            device_id={"gz": beside[side]},
            device_id_type=MESH,
        )

    def halo_start(turn, which, side):
        @pl.when(has[side])
        def _():
            halo(turn, which, side).start()

    def halo_arrived(turn, which, side):
        @pl.when(has[side])
        def _():
            halo(turn, which, 1 - side).wait_recv()

    def halo_sent(turn, which, side):
        @pl.when(has[side])
        def _():
            halo(turn, which, side).wait_send()

    def piece_copy(j):
        return pltpu.make_async_remote_copy(
            src_ref=courant_ref,
            dst_ref=pieces.at[j],
            send_sem=piece_send.at[j],
            recv_sem=piece_recv.at[j],
            device_id={"shot": partner(SPREAD - j)},
            device_id_type=MESH,
        )

    def back_copy(j):
        return pltpu.make_async_remote_copy(
            src_ref=outgoing.at[j],
            dst_ref=arriving.at[j],
            send_sem=back_send.at[j],
            recv_sem=back_recv.at[j],
            device_id={"shot": partner(j - SPREAD)},
            device_id_type=MESH,
        )

    for which in range(2):
        for side in range(2):
            halo_start(0, which, side)
    others = [j for j in range(SPAN) if j != SPREAD]
    for j in others:
        piece_copy(j).start()

    offset = offset_ref[0]
    by_y = banded(2 * across, across, across)
    by_x = banded(width, 2 * width, width)
    row = lax.broadcasted_iota(jnp.int32, (width * CHUNK, across), 0)
    place = (receivers_ref[0:1, :] - slab * depth) * width + receivers_ref[1:2, :]

    def mark(c, _):
        start = pl.multiple_of(c * CHUNK * width, CHUNK * width)
        hits[pl.ds(start, CHUNK * width), :] = jnp.where(row + start == place, 1.0, 0.0).astype(jnp.bfloat16)
        return 0

    lax.fori_loop(0, chunks, mark, 0)
    along = lax.broadcasted_iota(jnp.int32, (across, across), 0) == receivers_ref[2:3, :]
    for step in range(STEPS):
        high, low = in_two(jnp.where(along, traces_ref[step : step + 1, :], 0.0))
        amounts[step, :, 0:across] = high
        amounts[step, :, across : 2 * across] = low
    spot = jnp.where(
        (lax.broadcasted_iota(jnp.int32, (width, across), 0) == spot_ref[1])
        & (lax.broadcasted_iota(jnp.int32, (width, across), 1) == spot_ref[2]),
        1.0,
        0.0,
    )
    spot_depth = spot_ref[0] - slab * depth
    shown[pl.ds(0, 4)] = jnp.zeros((4, depth, WB, across), jnp.float32)
    shown[pl.ds(12, 4)] = jnp.zeros((4, depth, WB, across), jnp.float32)

    def stencil(buffer, which, z0):
        centre = fields[buffer, which, pl.ds(z0 + HALO, CHUNK)]
        high, low = in_two(centre)
        rows = CHUNK * width
        left = jnp.concatenate([high.reshape(rows, across), low.reshape(rows, across)], axis=1)
        in_y = jnp.dot(left, by_y, preferred_element_type=jnp.float32)
        right = jnp.concatenate(
            [
                jnp.concatenate([high[c] for c in range(CHUNK)], axis=1),
                jnp.concatenate([low[c] for c in range(CHUNK)], axis=1),
            ],
            axis=0,
        )
        in_x = jnp.dot(by_x, right, preferred_element_type=jnp.float32)
        result = []
        for c in range(CHUNK):
            total = CENTRE * centre[c] + in_y[c * width : (c + 1) * width] + in_x[:, c * across : (c + 1) * across]
            for k in range(1, 5):
                above = fields[buffer, which, z0 + HALO + c + k]
                below = fields[buffer, which, z0 + HALO + c - k]
                total = total + SIDE[k - 1] * (above + below)
            result.append(total)
        return centre, result

    def injected(step, z0):
        start = pl.multiple_of(z0 * width, CHUNK * width)
        found = hits[pl.ds(start, CHUNK * width), :]
        return lax.dot_general(
            jnp.concatenate([found, found], axis=1),
            amounts[step],
            (((1,), (1,)), ((), ())),
            preferred_element_type=jnp.float32,
        )

    def advance(step, which, z0, centre, lap):
        later = 1 - step % 2
        if which == 1:
            added = injected(step, z0)
        for c in range(CHUNK):
            if which == 0:
                extra = spot * jnp.where(z0 + c == spot_depth, wavelet_ref[step], 0.0)
            else:
                extra = added[c * width : (c + 1) * width]
            fields[later, which, z0 + HALO + c] = (
                2.0 * centre[c] - fields[later, which, z0 + HALO + c] + model[z0 + c] * lap[c] + extra
            )

    def see(step, z0, lap):
        now = step % 2
        for c in range(CHUNK):
            seen = fields[now, 1, z0 + HALO + c] * lap[c]
            if step > 0:
                seen = imaging[z0 + c] + seen
            if step < STEPS - 1:
                imaging[z0 + c] = seen
            else:
                weighted = taper_ref[...] * seen
                for s in range(WB):
                    shown[4 + s, z0 + c] = weighted[s * WB : (s + 1) * WB]

    def first_part(which, z0):
        _, lap = stencil(0, which, z0)
        for c in range(CHUNK):
            laps[which, z0 + c] = lap[c]
        if which == 0:
            see(0, z0, lap)

    def second_part(which, z0):
        centre = fields[0, which, pl.ds(z0 + HALO, CHUNK)]
        advance(0, which, z0, centre, [laps[which, z0 + c] for c in range(CHUNK)])

    def whole(step, which, z0):
        centre, lap = stencil(step % 2, which, z0)
        if which == 0:
            see(step, z0, lap)
        advance(step, which, z0, centre, lap)

    def inner(body):
        def turn(c, _):
            body(pl.multiple_of(c * CHUNK, CHUNK))
            return 0

        lax.fori_loop(1, chunks - 1, turn, 0)

    ends = (0, depth - CHUNK)
    for copy in loads[:2]:
        copy.wait()
    for which in range(2):
        inner(functools.partial(first_part, which))
    for which in range(2):
        for side in range(2):
            halo_arrived(0, which, side)
            first_part(which, ends[side])
    for copy in loads[2:]:
        copy.wait()
    for j in others:
        piece_copy(j).wait_recv()
    for s in range(WB):
        model[:, s * WB : (s + 1) * WB, :] = pieces[offset + SPREAD + s] * (1.0 / SCALE)
    for which in range(2):
        for side in range(2):
            second_part(which, ends[side])
            halo_start(1, which, side)
    for which in range(2):
        inner(functools.partial(second_part, which))

    for step in range(1, STEPS):
        for which in range(2):
            for side in range(2):
                halo_arrived(step, which, side)
                if step > 1:
                    halo_sent(step - 1, which, side)
                whole(step, which, ends[side])
                if step < STEPS - 1:
                    halo_start(step + 1, which, side)
            inner(functools.partial(whole, step, which))
            if step == STEPS - 1 and which == 0:
                field_copy = pltpu.make_async_copy(fields.at[0, 0, pl.ds(HALO, depth)], field_out, load_sem.at[0])
                field_copy.start()
                for j in range(SPAN):
                    outgoing[j] = shown[j + 2 - offset]
                    if j != SPREAD:
                        back_copy(j).start()
    adjoint_copy = pltpu.make_async_copy(fields.at[0, 1, pl.ds(HALO, depth)], adjoint_out, load_sem.at[1])
    adjoint_copy.start()
    for which in range(2):
        for side in range(2):
            halo_sent(0, which, side)
            halo_sent(STEPS - 1, which, side)
    for j in others:
        piece_copy(j).wait_send()
    for j in others:
        back_copy(j).wait_recv()

    def add_up(c, _):
        total = outgoing[SPREAD, pl.ds(c * CHUNK, CHUNK)]
        for j in others:
            total = total + arriving[j, pl.ds(c * CHUNK, CHUNK)]
        gradient[pl.ds(c * CHUNK, CHUNK)] = total
        return 0

    lax.fori_loop(0, chunks, add_up, 0)
    gradient_copy = pltpu.make_async_copy(gradient, gradient_out, load_sem.at[2])
    gradient_copy.start()
    for j in others:
        back_copy(j).wait_send()
    field_copy.wait()
    adjoint_copy.wait()
    gradient_copy.wait()


def per_device(
    squared_courant,
    window_offset,
    field_last,
    field_after,
    adjoint_last,
    adjoint_after,
    source_place,
    source_wavelet,
    receiver_place,
    receiver_trace,
):
    _, depth, width, across = field_last.shape
    x = np.arange(width)
    taper = (np.sin(math.pi * (x + 0.5) / width) ** 2 / SCALE).astype(np.float32)
    taper = jnp.asarray(np.broadcast_to(taper[:, None], (width, across)))
    smem = pl.BlockSpec(memory_space=pltpu.SMEM)
    vmem = pl.BlockSpec(memory_space=pltpu.VMEM)
    hbm = pl.BlockSpec(memory_space=pl.ANY)
    f32 = jnp.float32
    dma = pltpu.SemaphoreType.DMA
    field, adjoint, gradient = pl.pallas_call(
        kernel,
        out_shape=(
            jax.ShapeDtypeStruct((depth, width, across), f32),
            jax.ShapeDtypeStruct((depth, width, across), f32),
            jax.ShapeDtypeStruct((depth, WB, across), f32),
        ),
        in_specs=[smem] * 3 + [vmem] * 3 + [hbm] * 5,
        out_specs=(hbm, hbm, hbm),
        scratch_shapes=[
            pltpu.VMEM((2, 2, depth + 2 * HALO, width, across), f32),
            pltpu.VMEM((SPAN, depth, WB, across), f32),
            pltpu.VMEM((2, depth, width, across), f32),
            pltpu.VMEM((depth, width, across), f32),
            pltpu.VMEM((depth, width, across), f32),
            pltpu.VMEM((SPAN + 4, depth, WB, across), f32),
            pltpu.VMEM((SPAN, depth, WB, across), f32),
            pltpu.VMEM((SPAN, depth, WB, across), f32),
            pltpu.VMEM((depth, WB, across), f32),
            pltpu.VMEM((depth * width, across), jnp.bfloat16),
            pltpu.VMEM((STEPS, across, 2 * across), jnp.bfloat16),
            dma((5,)),
            dma((STEPS, 2, 2)),
            dma((STEPS, 2, 2)),
            dma((SPAN,)),
            dma((SPAN,)),
            dma((SPAN,)),
            dma((SPAN,)),
        ],
        compiler_params=pltpu.CompilerParams(
            collective_id=0, has_side_effects=True, vmem_limit_bytes=40 * 1024 * 1024
        ),
        name="inversion",
    )(
        window_offset,
        source_place[0],
        source_wavelet[0],
        receiver_place[0],
        receiver_trace[0],
        taper,
        squared_courant,
        field_last[0],
        field_after[0],
        adjoint_last[0],
        adjoint_after[0],
    )
    return field[None], adjoint[None], gradient


def solution(mesh):
    placed = (
        P("gz", "shot", None),
        P("shot"),
        P("shot", "gz", None, None),
        P("shot", "gz", None, None),
        P("shot", "gz", None, None),
        P("shot", "gz", None, None),
        P("shot", None),
        P("shot", None),
        P("shot", None, None),
        P("shot", None, None),
    )
    return jax.shard_map(
        per_device,
        mesh=mesh,
        in_specs=placed,
        out_specs=(P("shot", "gz", None, None), P("shot", "gz", None, None), P("gz", "shot", None)),
        check_vma=False,
    )
```

```python
import functools
import math

import jax
import jax.numpy as jnp
import numpy as np
from jax import lax
from jax.experimental import pallas as pl
from jax.experimental.pallas import tpu as pltpu
from jax.sharding import PartitionSpec as P

WB = 8
COLS = 4
FIRST = (0, 1, -2, -1)
SPREAD = 2
STEPS = 4
SPAN = WB + 2 * SPREAD
HALO = 4
CHUNK = 4
SCALE = 5040.0
CENTRE = -3.0 * 14350.0
SIDE = (8064.0, -1008.0, 128.0, -9.0)
MESH = pl.DeviceIdType.MESH


def banded(rows, cols, period):
    i = lax.broadcasted_iota(jnp.int32, (rows, cols), 0)
    j = lax.broadcasted_iota(jnp.int32, (rows, cols), 1)
    gap = jnp.abs(lax.rem(i, period) - lax.rem(j, period))
    band = jnp.zeros((rows, cols), jnp.float32)
    for k in range(1, 5):
        band = jnp.where(gap == k, SIDE[k - 1], band)
    return band.astype(jnp.bfloat16)


def in_two(values):
    high = values.astype(jnp.bfloat16)
    low = (values - high.astype(jnp.float32)).astype(jnp.bfloat16)
    return high, low


def kernel(
    offset_ref,
    spot_ref,
    wavelet_ref,
    receivers_in,
    traces_in,
    taper_in,
    courant_ref,
    field_last,
    field_after,
    adjoint_last,
    adjoint_after,
    field_out,
    adjoint_out,
    gradient_out,
    fields,
    pieces,
    laps,
    model,
    imaging,
    shown,
    outgoing,
    from_row,
    sums,
    from_rows,
    gradient,
    receivers_ref,
    traces_ref,
    taper_ref,
    hits,
    amounts,
    load_sem,
    halo_send,
    halo_recv,
    row_send,
    row_recv,
    piece_send,
    piece_recv,
    back_send,
    back_recv,
    sum_send,
    sum_recv,
):
    shot = lax.axis_index("shot")
    slab = lax.axis_index("gz")
    shots = lax.axis_size("shot")
    slabs = lax.axis_size("gz")
    depth, width, across = field_last.shape
    chunks = depth // CHUNK
    has = (slab > 0, slab < slabs - 1)
    beside = (jnp.maximum(slab - 1, 0), jnp.minimum(slab + 1, slabs - 1))

    row, col = shot // COLS, lax.rem(shot, COLS)
    rows = shots // COLS
    has_extra = col != 1
    extra_row = jnp.where(col == 0, 3, -1)

    def in_row(dx):
        return row * COLS + lax.rem(col + dx, COLS)

    def in_column(r):
        return lax.rem(row + r + rows, rows) * COLS + col

    def first_row(source, dx):
        return (source + FIRST[dx] - lax.rem(source + dx, COLS)) // COLS

    loads = []
    for i, (buffer, which, source) in enumerate(
        ((0, 0, field_last), (0, 1, adjoint_last), (1, 0, field_after), (1, 1, adjoint_after))
    ):
        loads.append(pltpu.make_async_copy(source, fields.at[buffer, which, pl.ds(HALO, depth)], load_sem.at[i]))
    for i, (source, place) in enumerate(
        (
            (courant_ref, pieces.at[SPREAD]),
            (receivers_in, receivers_ref),
            (traces_in, traces_ref),
            (taper_in, taper_ref),
        )
    ):
        loads.append(pltpu.make_async_copy(source, place, load_sem.at[4 + i]))
    for copy in loads:
        copy.start()

    blank = jnp.zeros((HALO, width, across), jnp.float32)
    for side, place in ((0, 0), (1, HALO + depth)):

        @pl.when(jnp.logical_not(has[side]))
        def _():
            for buffer in range(2):
                for which in range(2):
                    fields[buffer, which, pl.ds(place, HALO)] = blank

    barrier = pltpu.get_barrier_semaphore()
    for dx in range(1, COLS):
        pl.semaphore_signal(barrier, inc=1, device_id={"shot": in_row(dx)}, device_id_type=MESH)
    for r in (-3, -2, -1, 1, 2, 3):
        pl.semaphore_signal(barrier, inc=1, device_id={"shot": in_column(r)}, device_id_type=MESH)
    for side in range(2):

        @pl.when(has[side])
        def _():
            pl.semaphore_signal(barrier, inc=1, device_id={"gz": beside[side]}, device_id_type=MESH)

    beside_count = jnp.where(has[0], 1, 0) + jnp.where(has[1], 1, 0)
    pl.semaphore_wait(barrier, COLS - 1 + 6 + beside_count)

    def halo(turn, which, side):
        place = HALO if side == 0 else depth
        landing = HALO + depth if side == 0 else 0
        if turn == 0:
            source = (field_last, adjoint_last)[which].at[pl.ds(place - HALO, HALO)]
        else:
            source = fields.at[turn % 2, which, pl.ds(place, HALO)]
        return pltpu.make_async_remote_copy(
            src_ref=source,
            dst_ref=fields.at[turn % 2, which, pl.ds(landing, HALO)],
            send_sem=halo_send.at[turn, which, side],
            recv_sem=halo_recv.at[turn, which, side],
            device_id={"gz": beside[side]},
            device_id_type=MESH,
        )

    def halo_start(turn, which, side):
        @pl.when(has[side])
        def _():
            halo(turn, which, side).start()

    def halo_arrived(turn, which, side):
        @pl.when(has[side])
        def _():
            halo(turn, which, 1 - side).wait_recv()

    def halo_sent(turn, which, side):
        @pl.when(has[side])
        def _():
            halo(turn, which, side).wait_send()

    def row_copy(i):
        return pltpu.make_async_remote_copy(
            src_ref=courant_ref,
            dst_ref=pieces.at[(SPREAD + COLS, SPREAD + 2 * COLS, SPAN)[i]],
            send_sem=row_send.at[i],
            recv_sem=row_recv.at[i],
            device_id={"shot": in_column((-1, -2, -extra_row)[i])},
            device_id_type=MESH,
        )

    def piece_copy(dx, r):
        target = lax.rem(col + dx, COLS)
        slot = COLS * r + col - target + SPREAD
        held = jnp.where((r >= 0) & (r <= 2), SPREAD + COLS * r, SPAN)
        return pltpu.make_async_remote_copy(
            src_ref=pieces.at[held],
            dst_ref=pieces.at[slot],
            send_sem=piece_send.at[dx - 1, r - slab_row(dx)],
            recv_sem=piece_recv.at[slot],
            device_id={"shot": in_row(dx)},
            device_id_type=MESH,
        )

    def slab_row(dx):
        return first_row(lax.rem(col + dx, COLS), COLS - dx)

    def piece_arrived(j):
        pltpu.make_async_copy(pieces.at[j], pieces.at[j], piece_recv.at[j]).wait()

    def part_copy(dx, r):
        target = lax.rem(col + dx, COLS)
        return pltpu.make_async_remote_copy(
            src_ref=outgoing.at[COLS * r + target - col + SPREAD],
            dst_ref=from_row.at[dx - 1, r - first_row(col, dx)],
            send_sem=back_send.at[dx - 1, r - first_row(col, dx)],
            recv_sem=back_recv.at[dx - 1, r - first_row(col, dx)],
            device_id={"shot": in_row(dx)},
            device_id_type=MESH,
        )

    def part_start(dx, r):
        first = first_row(col, dx)

        @pl.when((r >= first) & (r <= first + 2))
        def _():
            part_copy(dx, r).start()

    def source_row(dx):
        return first_row(lax.rem(col - dx + COLS, COLS), dx)

    def part_arrived(dx, r):
        first = source_row(dx)

        @pl.when((r >= first) & (r <= first + 2))
        def _():
            place = from_row.at[dx - 1, r - first]
            pltpu.make_async_copy(place, place, back_recv.at[dx - 1, r - first]).wait()

    def summed(r, own, c):
        place = pl.ds(pl.multiple_of(c * CHUNK, CHUNK), CHUNK)
        total = outgoing[SPREAD + COLS * r, place] if own else jnp.zeros((CHUNK, WB, across), jnp.float32)
        for dx in range(1, COLS):
            at = r - source_row(dx)
            total = total + from_row[dx - 1, jnp.where((at >= 0) & (at <= 2), at, 3), place]
        return total

    def sum_copy(i):
        return pltpu.make_async_remote_copy(
            src_ref=sums.at[i],
            dst_ref=from_rows.at[i],
            send_sem=sum_send.at[i],
            recv_sem=sum_recv.at[i],
            device_id={"shot": in_column((1, 2, extra_row)[i])},
            device_id_type=MESH,
        )

    def sum_start(i):
        r = (1, 2, extra_row)[i]
        for dx in range(1, COLS):
            part_arrived(dx, r)

        def turn(c, _):
            sums[i, pl.ds(pl.multiple_of(c * CHUNK, CHUNK), CHUNK)] = summed(r, i < 2, c)
            return 0

        lax.fori_loop(0, chunks, turn, 0)
        sum_copy(i).start()

    for which in range(2):
        for side in range(2):
            halo_start(0, which, side)
    row_copy(0).start()

    @pl.when(has_extra)
    def _():
        row_copy(2).start()

    row_copy(1).start()
    own_slab = loads.pop(4)
    own_slab.wait()
    for dx in range(1, COLS):

        @pl.when(slab_row(dx) <= 0)
        def _():
            piece_copy(dx, 0).start()


    offset = offset_ref[0]
    for copy in loads[4:]:
        copy.wait()
    by_y = banded(2 * across, across, across)
    by_x = banded(width, 2 * width, width)
    cell = lax.broadcasted_iota(jnp.int32, (width * CHUNK, across), 0)
    place = (receivers_ref[0] - slab * depth) * width + receivers_ref[1]

    def mark(c, _):
        start = pl.multiple_of(c * CHUNK * width, CHUNK * width)
        hits[pl.ds(start, CHUNK * width), :] = jnp.where(cell + start == place, 1.0, 0.0).astype(jnp.bfloat16)
        return 0

    lax.fori_loop(0, chunks, mark, 0)
    along = lax.broadcasted_iota(jnp.int32, (across, across), 0) == receivers_ref[2]
    for step in range(STEPS):
        high, low = in_two(jnp.where(along, traces_ref[step : step + 1, :], 0.0))
        amounts[step, :, 0:across] = high
        amounts[step, :, across : 2 * across] = low
    spot = jnp.where(
        (lax.broadcasted_iota(jnp.int32, (width, across), 0) == spot_ref[1])
        & (lax.broadcasted_iota(jnp.int32, (width, across), 1) == spot_ref[2]),
        1.0,
        0.0,
    )
    spot_depth = spot_ref[0] - slab * depth
    shown[pl.ds(0, 4)] = jnp.zeros((4, depth, WB, across), jnp.float32)
    shown[pl.ds(12, 4)] = jnp.zeros((4, depth, WB, across), jnp.float32)

    def stencil(buffer, which, z0):
        centre = fields[buffer, which, pl.ds(z0 + HALO, CHUNK)]
        high, low = in_two(centre)
        rows = CHUNK * width
        left = jnp.concatenate([high.reshape(rows, across), low.reshape(rows, across)], axis=1)
        in_y = jnp.dot(left, by_y, preferred_element_type=jnp.float32)
        right = jnp.concatenate(
            [
                jnp.concatenate([high[c] for c in range(CHUNK)], axis=1),
                jnp.concatenate([low[c] for c in range(CHUNK)], axis=1),
            ],
            axis=0,
        )
        in_x = jnp.dot(by_x, right, preferred_element_type=jnp.float32)
        result = []
        for c in range(CHUNK):
            total = CENTRE * centre[c] + in_y[c * width : (c + 1) * width] + in_x[:, c * across : (c + 1) * across]
            for k in range(1, 5):
                above = fields[buffer, which, z0 + HALO + c + k]
                below = fields[buffer, which, z0 + HALO + c - k]
                total = total + SIDE[k - 1] * (above + below)
            result.append(total)
        return centre, result

    def injected(step, z0):
        start = pl.multiple_of(z0 * width, CHUNK * width)
        found = hits[pl.ds(start, CHUNK * width), :]
        return lax.dot_general(
            jnp.concatenate([found, found], axis=1),
            amounts[step],
            (((1,), (1,)), ((), ())),
            preferred_element_type=jnp.float32,
        )

    def advance(step, which, z0, centre, lap):
        later = 1 - step % 2
        if which == 1:
            added = injected(step, z0)
        for c in range(CHUNK):
            if which == 0:
                extra = spot * jnp.where(z0 + c == spot_depth, wavelet_ref[step], 0.0)
            else:
                extra = added[c * width : (c + 1) * width]
            fields[later, which, z0 + HALO + c] = (
                2.0 * centre[c] - fields[later, which, z0 + HALO + c] + model[z0 + c] * lap[c] + extra
            )

    def see(step, z0, lap):
        now = step % 2
        for c in range(CHUNK):
            seen = fields[now, 1, z0 + HALO + c] * lap[c]
            if step > 0:
                seen = imaging[z0 + c] + seen
            if step < STEPS - 1:
                imaging[z0 + c] = seen
            else:
                weighted = taper_ref[...] * seen
                for s in range(WB):
                    shown[4 + s, z0 + c] = weighted[s * WB : (s + 1) * WB]

    def first_part(which, z0):
        _, lap = stencil(0, which, z0)
        for c in range(CHUNK):
            laps[which, z0 + c] = lap[c]
        if which == 0:
            see(0, z0, lap)

    def second_part(which, z0):
        centre = fields[0, which, pl.ds(z0 + HALO, CHUNK)]
        advance(0, which, z0, centre, [laps[which, z0 + c] for c in range(CHUNK)])

    def whole(step, which, z0):
        centre, lap = stencil(step % 2, which, z0)
        if which == 0:
            see(step, z0, lap)
        advance(step, which, z0, centre, lap)

    def inner(body):
        def turn(c, _):
            body(pl.multiple_of(c * CHUNK, CHUNK))
            return 0

        lax.fori_loop(1, chunks - 1, turn, 0)

    def pass_on_near():
        row_copy(0).wait_recv()
        for dx in (1, 3, 2):
            piece_copy(dx, 1).start()

        @pl.when(has_extra)
        def _():
            row_copy(2).wait_recv()

        for dx in range(1, COLS):
            first = slab_row(dx)

            @pl.when(first != 0)
            def _():
                piece_copy(dx, jnp.where(first < 0, -1, 3)).start()

    def pass_on_later():
        row_copy(1).wait_recv()
        for dx in range(1, COLS):

            @pl.when(slab_row(dx) >= 0)
            def _():
                piece_copy(dx, 2).start()

    ends = (0, depth - CHUNK)
    for copy in loads[:2]:
        copy.wait()
    inner(functools.partial(first_part, 0))
    pass_on_near()
    inner(functools.partial(first_part, 1))
    for which in range(2):
        for side in range(2):
            halo_arrived(0, which, side)
            first_part(which, ends[side])
    for copy in loads[2:4]:
        copy.wait()
    pass_on_later()
    for j in range(SPAN):
        if j % COLS != SPREAD:
            piece_arrived(j)
    for s in range(WB):
        model[:, s * WB : (s + 1) * WB, :] = pieces[offset + SPREAD + s] * (1.0 / SCALE)
    for which in range(2):
        for side in range(2):
            second_part(which, ends[side])
            halo_start(1, which, side)
    for which in range(2):
        inner(functools.partial(second_part, which))

    for step in range(1, STEPS):
        for which in range(2):
            for side in range(2):
                halo_arrived(step, which, side)
                if step > 1:
                    halo_sent(step - 1, which, side)
                whole(step, which, ends[side])
                if step < STEPS - 1:
                    halo_start(step + 1, which, side)
            inner(functools.partial(whole, step, which))
            if step == STEPS - 1 and which == 0:
                field_copy = pltpu.make_async_copy(fields.at[0, 0, pl.ds(HALO, depth)], field_out, load_sem.at[0])
                field_copy.start()
                for j in range(SPAN):
                    outgoing[j] = shown[j + 2 - offset]
                for r in (2, -1, 3, 1, 0):
                    for dx in (1, 3, 2):
                        part_start(dx, r)
                from_row[:, 3] = jnp.zeros((COLS - 1, depth, WB, across), jnp.float32)
    adjoint_copy = pltpu.make_async_copy(fields.at[0, 1, pl.ds(HALO, depth)], adjoint_out, load_sem.at[1])
    adjoint_copy.start()
    sum_start(1)

    @pl.when(has_extra)
    def _():
        sum_start(2)

    sum_start(0)
    for dx in range(1, COLS):
        part_arrived(dx, 0)
    for i in (0, 1):
        sum_copy(i).wait_recv()

    @pl.when(has_extra)
    def _():
        sum_copy(2).wait_recv()

    @pl.when(jnp.logical_not(has_extra))
    def _():
        from_rows[2] = jnp.zeros((depth, WB, across), jnp.float32)

    def add_up(c, _):
        place = pl.ds(pl.multiple_of(c * CHUNK, CHUNK), CHUNK)
        gradient[place] = summed(0, True, c) + from_rows[0, place] + from_rows[1, place] + from_rows[2, place]
        return 0

    lax.fori_loop(0, chunks, add_up, 0)
    gradient_copy = pltpu.make_async_copy(gradient, gradient_out, load_sem.at[2])
    gradient_copy.start()
    for which in range(2):
        for side in range(2):
            halo_sent(0, which, side)
            halo_sent(STEPS - 1, which, side)
    for i in (0, 1):
        row_copy(i).wait_send()
        sum_copy(i).wait_send()

    @pl.when(has_extra)
    def _():
        row_copy(2).wait_send()
        sum_copy(2).wait_send()

    for dx in range(1, COLS):
        for t in range(3):
            piece_copy(dx, slab_row(dx) + t).wait_send()
            part_copy(dx, first_row(col, dx) + t).wait_send()
    field_copy.wait()
    adjoint_copy.wait()
    gradient_copy.wait()


def per_device(
    squared_courant,
    window_offset,
    field_last,
    field_after,
    adjoint_last,
    adjoint_after,
    source_place,
    source_wavelet,
    receiver_place,
    receiver_trace,
):
    _, depth, width, across = field_last.shape
    x = np.arange(width)
    taper = (np.sin(math.pi * (x + 0.5) / width) ** 2 / SCALE).astype(np.float32)
    taper = jnp.asarray(np.broadcast_to(taper[:, None], (width, across)))
    smem = pl.BlockSpec(memory_space=pltpu.SMEM)
    hbm = pl.BlockSpec(memory_space=pl.ANY)
    f32 = jnp.float32
    dma = pltpu.SemaphoreType.DMA
    field, adjoint, gradient = pl.pallas_call(
        kernel,
        out_shape=(
            jax.ShapeDtypeStruct((depth, width, across), f32),
            jax.ShapeDtypeStruct((depth, width, across), f32),
            jax.ShapeDtypeStruct((depth, WB, across), f32),
        ),
        in_specs=[smem] * 3 + [hbm] * 8,
        out_specs=(hbm, hbm, hbm),
        scratch_shapes=[
            pltpu.VMEM((2, 2, depth + 2 * HALO, width, across), f32),
            pltpu.VMEM((SPAN + 1, depth, WB, across), f32),
            pltpu.VMEM((2, depth, width, across), f32),
            pltpu.VMEM((depth, width, across), f32),
            pltpu.VMEM((depth, width, across), f32),
            pltpu.VMEM((SPAN + 4, depth, WB, across), f32),
            pltpu.VMEM((SPAN, depth, WB, across), f32),
            pltpu.VMEM((COLS - 1, 4, depth, WB, across), f32),
            pltpu.VMEM((3, depth, WB, across), f32),
            pltpu.VMEM((3, depth, WB, across), f32),
            pltpu.VMEM((depth, WB, across), f32),
            pltpu.VMEM((3, 1, across), jnp.int32),
            pltpu.VMEM((STEPS, across), f32),
            pltpu.VMEM((width, across), f32),
            pltpu.VMEM((depth * width, across), jnp.bfloat16),
            pltpu.VMEM((STEPS, across, 2 * across), jnp.bfloat16),
            dma((8,)),
            dma((STEPS, 2, 2)),
            dma((STEPS, 2, 2)),
            dma((3,)),
            dma((3,)),
            dma((COLS - 1, 3)),
            dma((SPAN,)),
            dma((COLS - 1, 3)),
            dma((COLS - 1, 3)),
            dma((3,)),
            dma((3,)),
        ],
        compiler_params=pltpu.CompilerParams(
            collective_id=0, has_side_effects=True, vmem_limit_bytes=56 * 1024 * 1024
        ),
        name="inversion",
    )(
        window_offset,
        source_place[0],
        source_wavelet[0],
        receiver_place.transpose(1, 0, 2),
        receiver_trace[0],
        taper,
        squared_courant,
        field_last[0],
        field_after[0],
        adjoint_last[0],
        adjoint_after[0],
    )
    return field[None], adjoint[None], gradient


def solution(mesh):
    placed = (
        P("gz", "shot", None),
        P("shot"),
        P("shot", "gz", None, None),
        P("shot", "gz", None, None),
        P("shot", "gz", None, None),
        P("shot", "gz", None, None),
        P("shot", None),
        P("shot", None),
        P("shot", None, None),
        P("shot", None, None),
    )
    return jax.shard_map(
        per_device,
        mesh=mesh,
        in_specs=placed,
        out_specs=(P("shot", "gz", None, None), P("shot", "gz", None, None), P("gz", "shot", None)),
        check_vma=False,
    )
```

```python
import functools
import math

import jax
import jax.numpy as jnp
from jax import lax
from jax.experimental import pallas as pl
from jax.experimental.pallas import tpu as pltpu
from jax.sharding import PartitionSpec as P

WB = 8
COLS = 4
FIRST = (0, 1, -2, -1)
SPREAD = 2
STEPS = 4
SPAN = WB + 2 * SPREAD
HALO = 4
CHUNK = 4
BLOCK = 12
SCALE = 5040.0
CENTRE = -3.0 * 14350.0
SIDE = (8064.0, -1008.0, 128.0, -9.0)
MESH = pl.DeviceIdType.MESH


def banded(rows, cols, period):
    i = lax.broadcasted_iota(jnp.int32, (rows, cols), 0)
    j = lax.broadcasted_iota(jnp.int32, (rows, cols), 1)
    gap = jnp.abs(lax.rem(i, period) - lax.rem(j, period))
    band = jnp.zeros((rows, cols), jnp.float32)
    for k in range(1, 5):
        band = jnp.where(gap == k, SIDE[k - 1], band)
    return band.astype(jnp.bfloat16)


def in_two(values):
    high = values.astype(jnp.bfloat16)
    low = (values - high.astype(jnp.float32)).astype(jnp.bfloat16)
    return high, low


def kernel(
    offset_ref,
    spot_ref,
    wavelet_ref,
    receivers_in,
    traces_in,
    courant_ref,
    field_last,
    field_after,
    adjoint_last,
    adjoint_after,
    field_out,
    adjoint_out,
    gradient_out,
    field_a,
    adjoint_a,
    field_b,
    adjoint_b,
    pieces,
    laps,
    model,
    imaging,
    shown,
    outgoing,
    from_row,
    sums,
    from_rows,
    receivers_ref,
    traces_ref,
    taper_ref,
    hits,
    amounts,
    load_sem,
    halo_send,
    halo_recv,
    row_send,
    row_recv,
    piece_send,
    piece_recv,
    back_send,
    back_recv,
    sum_send,
    sum_recv,
):
    fields = ((field_a, adjoint_a), (field_b, adjoint_b))
    shot = lax.axis_index("shot")
    slab = lax.axis_index("gz")
    shots = lax.axis_size("shot")
    slabs = lax.axis_size("gz")
    depth, width, across = field_last.shape
    chunks = depth // CHUNK
    has = (slab > 0, slab < slabs - 1)
    beside = (jnp.maximum(slab - 1, 0), jnp.minimum(slab + 1, slabs - 1))

    row, col = shot // COLS, lax.rem(shot, COLS)
    rows = shots // COLS
    has_extra = col != 1
    extra_row = jnp.where(col == 0, 3, -1)

    def in_row(dx):
        return row * COLS + lax.rem(col + dx, COLS)

    def in_column(r):
        return lax.rem(row + r + rows, rows) * COLS + col

    def first_row(source, dx):
        return (source + FIRST[dx] - lax.rem(source + dx, COLS)) // COLS

    loads = []
    for i, (buffer, which, source) in enumerate(
        ((0, 0, field_last), (0, 1, adjoint_last), (1, 0, field_after), (1, 1, adjoint_after))
    ):
        loads.append(pltpu.make_async_copy(source, fields[buffer][which].at[pl.ds(HALO, depth)], load_sem.at[i]))
    for i, (source, place) in enumerate(
        (
            (courant_ref, pieces.at[SPREAD]),
            (receivers_in, receivers_ref),
            (traces_in, traces_ref),
        )
    ):
        loads.append(pltpu.make_async_copy(source, place, load_sem.at[4 + i]))
    for copy in loads:
        copy.start()

    blank = jnp.zeros((HALO, width, across), jnp.float32)
    for side, place in ((0, 0), (1, HALO + depth)):

        @pl.when(jnp.logical_not(has[side]))
        def _():
            for buffer in range(2):
                for which in range(2):
                    fields[buffer][which][pl.ds(place, HALO)] = blank

    barrier = pltpu.get_barrier_semaphore()
    for dx in range(1, COLS):
        pl.semaphore_signal(barrier, inc=1, device_id={"shot": in_row(dx)}, device_id_type=MESH)
    for r in (-3, -2, -1, 1, 2, 3):
        pl.semaphore_signal(barrier, inc=1, device_id={"shot": in_column(r)}, device_id_type=MESH)
    for side in range(2):

        @pl.when(has[side])
        def _():
            pl.semaphore_signal(barrier, inc=1, device_id={"gz": beside[side]}, device_id_type=MESH)

    beside_count = jnp.where(has[0], 1, 0) + jnp.where(has[1], 1, 0)
    pl.semaphore_wait(barrier, COLS - 1 + 6 + beside_count)

    def halo(turn, which, side):
        place = HALO if side == 0 else depth
        landing = HALO + depth if side == 0 else 0
        if turn == 0:
            source = (field_last, adjoint_last)[which].at[pl.ds(place - HALO, HALO)]
        else:
            source = fields[turn % 2][which].at[pl.ds(place, HALO)]
        return pltpu.make_async_remote_copy(
            src_ref=source,
            dst_ref=fields[turn % 2][which].at[pl.ds(landing, HALO)],
            send_sem=halo_send.at[turn, which, side],
            recv_sem=halo_recv.at[turn, which, side],
            device_id={"gz": beside[side]},
            device_id_type=MESH,
        )

    def halo_start(turn, which, side):
        @pl.when(has[side])
        def _():
            halo(turn, which, side).start()

    def halo_arrived(turn, which, side):
        @pl.when(has[side])
        def _():
            halo(turn, which, 1 - side).wait_recv()

    def halo_sent(turn, which, side):
        @pl.when(has[side])
        def _():
            halo(turn, which, side).wait_send()

    def row_copy(i):
        return pltpu.make_async_remote_copy(
            src_ref=courant_ref,
            dst_ref=pieces.at[(SPREAD + COLS, SPREAD + 2 * COLS, SPAN)[i]],
            send_sem=row_send.at[i],
            recv_sem=row_recv.at[i],
            device_id={"shot": in_column((-1, -2, -extra_row)[i])},
            device_id_type=MESH,
        )

    def piece_copy(dx, r):
        target = lax.rem(col + dx, COLS)
        slot = COLS * r + col - target + SPREAD
        held = jnp.where((r >= 0) & (r <= 2), SPREAD + COLS * r, SPAN)
        return pltpu.make_async_remote_copy(
            src_ref=pieces.at[held],
            dst_ref=pieces.at[slot],
            send_sem=piece_send.at[dx - 1, r - slab_row(dx)],
            recv_sem=piece_recv.at[slot],
            device_id={"shot": in_row(dx)},
            device_id_type=MESH,
        )

    def slab_row(dx):
        return first_row(lax.rem(col + dx, COLS), COLS - dx)

    def piece_arrived(j):
        pltpu.make_async_copy(pieces.at[j], pieces.at[j], piece_recv.at[j]).wait()

    def part_copy(dx, r):
        target = lax.rem(col + dx, COLS)
        return pltpu.make_async_remote_copy(
            src_ref=outgoing.at[COLS * r + target - col + SPREAD],
            dst_ref=from_row.at[dx - 1, r - first_row(col, dx)],
            send_sem=back_send.at[dx - 1, r - first_row(col, dx)],
            recv_sem=back_recv.at[dx - 1, r - first_row(col, dx)],
            device_id={"shot": in_row(dx)},
            device_id_type=MESH,
        )

    def part_start(dx, r):
        first = first_row(col, dx)

        @pl.when((r >= first) & (r <= first + 2))
        def _():
            part_copy(dx, r).start()

    def source_row(dx):
        return first_row(lax.rem(col - dx + COLS, COLS), dx)

    def part_arrived(dx, r):
        first = source_row(dx)

        @pl.when((r >= first) & (r <= first + 2))
        def _():
            place = from_row.at[dx - 1, r - first]
            pltpu.make_async_copy(place, place, back_recv.at[dx - 1, r - first]).wait()

    def summed(r, own, c):
        place = pl.ds(pl.multiple_of(c * CHUNK, CHUNK), CHUNK)
        total = outgoing[SPREAD + COLS * r, place] if own else jnp.zeros((CHUNK, WB, across), jnp.float32)
        for dx in range(1, COLS):
            at = r - source_row(dx)
            total = total + from_row[dx - 1, jnp.where((at >= 0) & (at <= 2), at, 3), place]
        return total

    def sum_copy(i):
        return pltpu.make_async_remote_copy(
            src_ref=sums.at[i],
            dst_ref=from_rows.at[i],
            send_sem=sum_send.at[i],
            recv_sem=sum_recv.at[i],
            device_id={"shot": in_column((1, 2, extra_row)[i])},
            device_id_type=MESH,
        )

    def sum_start(i):
        r = (1, 2, extra_row)[i]
        for dx in range(1, COLS):
            part_arrived(dx, r)

        def turn(c, _):
            sums[i, pl.ds(pl.multiple_of(c * CHUNK, CHUNK), CHUNK)] = summed(r, i < 2, c)
            return 0

        lax.fori_loop(0, chunks, turn, 0)
        sum_copy(i).start()

    for which in range(2):
        for side in range(2):
            halo_start(0, which, side)
    row_copy(0).start()

    @pl.when(has_extra)
    def _():
        row_copy(2).start()

    row_copy(1).start()
    own_slab = loads.pop(4)
    own_slab.wait()
    for dx in range(1, COLS):

        @pl.when(slab_row(dx) <= 0)
        def _():
            piece_copy(dx, 0).start()


    offset = offset_ref[0]
    for copy in loads[4:]:
        copy.wait()
    by_y = banded(2 * across, across, across)
    by_x = banded(width, 2 * width, width)
    cell = lax.broadcasted_iota(jnp.int32, (width * CHUNK, across), 0)
    place = (receivers_ref[0] - slab * depth) * width + receivers_ref[1]

    def mark(c, _):
        start = pl.multiple_of(c * CHUNK * width, CHUNK * width)
        hits[pl.ds(start, CHUNK * width), :] = jnp.where(cell + start == place, 1.0, 0.0).astype(jnp.bfloat16)
        return 0

    lax.fori_loop(0, chunks, mark, 0)
    along = lax.broadcasted_iota(jnp.int32, (across, across), 0) == receivers_ref[2]
    for step in range(STEPS):
        high, low = in_two(jnp.where(along, traces_ref[step : step + 1, :], 0.0))
        amounts[step, :, 0:across] = high
        amounts[step, :, across : 2 * across] = low
    across_x = lax.broadcasted_iota(jnp.int32, (width, across), 0).astype(jnp.float32)
    taper_ref[...] = jnp.sin((across_x + 0.5) * (math.pi / width)) ** 2 * (1.0 / SCALE)
    spot = jnp.where(
        (lax.broadcasted_iota(jnp.int32, (width, across), 0) == spot_ref[1])
        & (lax.broadcasted_iota(jnp.int32, (width, across), 1) == spot_ref[2]),
        1.0,
        0.0,
    )
    spot_depth = spot_ref[0] - slab * depth
    shown[pl.ds(0, 4)] = jnp.zeros((4, depth, WB, across), jnp.float32)
    shown[pl.ds(12, 4)] = jnp.zeros((4, depth, WB, across), jnp.float32)

    def flat(high, low, planes):
        rows = planes * width
        left = jnp.concatenate([high.reshape(rows, across), low.reshape(rows, across)], axis=1)
        in_y = jnp.dot(left, by_y, preferred_element_type=jnp.float32)
        right = jnp.concatenate(
            [jnp.concatenate([part[c] for c in range(planes)], axis=1) for part in (high, low)], axis=0
        )
        in_x = jnp.dot(by_x, right, preferred_element_type=jnp.float32)
        return in_y, in_x

    def spans(starts, planes):
        return [(z0, i * planes) for i, z0 in enumerate(starts)]

    def injected(step, starts, planes):
        found = []
        for z0 in starts:
            found.append(hits[pl.ds(pl.multiple_of(z0 * width, CHUNK * width), planes * width), :])
        found = jnp.concatenate(found, axis=0)
        return lax.dot_general(
            jnp.concatenate([found, found], axis=1),
            amounts[step],
            (((1,), (1,)), ((), ())),
            preferred_element_type=jnp.float32,
        )

    def laplace(now, starts, planes, use):
        high, low = in_two(jnp.concatenate([now[pl.ds(z0 + HALO, planes)] for z0 in starts], axis=0))
        in_y, in_x = flat(high, low, planes * len(starts))
        for s in range(width // WB):
            tile = pl.ds(s * WB, WB)
            for z0, first in spans(starts, planes):
                line = [now[z0 + c, tile] for c in range(planes + 2 * HALO)]
                for c in range(planes):
                    at = first + c
                    centre = line[c + HALO]
                    total = CENTRE * centre + in_y[at * width + s * WB : at * width + (s + 1) * WB]
                    total = total + in_x[s * WB : (s + 1) * WB, at * across : (at + 1) * across]
                    for k in range(1, 5):
                        total = total + SIDE[k - 1] * (line[c + HALO + k] + line[c + HALO - k])
                    use(z0 + c, at, s, tile, centre, total)

    def see(step, z, s, tile, lap):
        seen = fields[step % 2][1][z + HALO, tile] * lap
        if step > 0:
            seen = imaging[z, tile] + seen
        if step < STEPS - 1:
            imaging[z, tile] = seen
        else:
            shown[4 + s, z] = taper_ref[tile] * seen

    def advance(step, which, z, tile, centre, lap, extra):
        later = fields[1 - step % 2][which]
        new = 2.0 * centre - later[z + HALO, tile] + model[z, tile] * lap + extra
        if step < STEPS - 1:
            later[z + HALO, tile] = new
        else:
            (field_out, adjoint_out)[which][z, tile] = new

    def extras(step, which, starts, planes):
        if which == 0:
            return lambda z, at, s, tile: spot[s * WB : (s + 1) * WB] * jnp.where(
                z == spot_depth, wavelet_ref[step], 0.0
            )
        added = injected(step, starts, planes)
        return lambda z, at, s, tile: added[at * width + s * WB : at * width + (s + 1) * WB]

    def first_part(which, starts, planes):
        def use(z, at, s, tile, centre, lap):
            laps[which, z, tile] = lap
            if which == 0:
                see(0, z, s, tile, lap)

        laplace(fields[0][which], starts, planes, use)

    def second_part(which, starts, planes):
        extra = extras(0, which, starts, planes)
        for s in range(width // WB):
            tile = pl.ds(s * WB, WB)
            for z0, first in spans(starts, planes):
                for c in range(planes):
                    z = z0 + c
                    centre = fields[0][which][z + HALO, tile]
                    advance(0, which, z, tile, centre, laps[which, z, tile], extra(z, first + c, s, tile))

    def whole(step, which, starts, planes):
        extra = extras(step, which, starts, planes)

        def use(z, at, s, tile, centre, lap):
            if which == 0:
                see(step, z, s, tile, lap)
            advance(step, which, z, tile, centre, lap, extra(z, at, s, tile))

        laplace(fields[step % 2][which], starts, planes, use)

    def inner(body):
        def turn(c, _):
            body([pl.multiple_of(c * BLOCK + HALO, CHUNK)], BLOCK)
            return 0

        lax.fori_loop(0, (depth - 2 * HALO) // BLOCK, turn, 0)

    def pass_on_near():
        row_copy(0).wait_recv()
        for dx in (1, 3, 2):
            piece_copy(dx, 1).start()

        @pl.when(has_extra)
        def _():
            row_copy(2).wait_recv()

        for dx in range(1, COLS):
            first = slab_row(dx)

            @pl.when(first != 0)
            def _():
                piece_copy(dx, jnp.where(first < 0, -1, 3)).start()

    def pass_on_later():
        row_copy(1).wait_recv()
        for dx in range(1, COLS):

            @pl.when(slab_row(dx) >= 0)
            def _():
                piece_copy(dx, 2).start()

    ends = (0, depth - CHUNK)
    for copy in loads[:2]:
        copy.wait()
    inner(functools.partial(first_part, 0))
    pass_on_near()
    inner(functools.partial(first_part, 1))
    for which in range(2):
        for side in range(2):
            halo_arrived(0, which, side)
        first_part(which, ends, CHUNK)
    for copy in loads[2:4]:
        copy.wait()
    pass_on_later()
    for j in range(SPAN):
        if j % COLS != SPREAD:
            piece_arrived(j)
    for s in range(WB):
        model[:, s * WB : (s + 1) * WB, :] = pieces[offset + SPREAD + s] * (1.0 / SCALE)
    for which in range(2):
        second_part(which, ends, CHUNK)
        for side in range(2):
            halo_start(1, which, side)
    for which in range(2):
        inner(functools.partial(second_part, which))

    for step in range(1, STEPS):
        for which in range(2):
            for side in range(2):
                halo_arrived(step, which, side)
                if step > 1:
                    halo_sent(step - 1, which, side)
            whole(step, which, ends, CHUNK)
            if step < STEPS - 1:
                for side in range(2):
                    halo_start(step + 1, which, side)
            inner(functools.partial(whole, step, which))
            if step == STEPS - 1 and which == 0:
                for j in range(SPAN):
                    outgoing[j] = shown[j + 2 - offset]
                for r in (2, -1, 3, 1, 0):
                    for dx in (1, 3, 2):
                        part_start(dx, r)
                from_row[:, 3] = jnp.zeros((COLS - 1, depth, WB, across), jnp.float32)
    sum_start(1)

    @pl.when(has_extra)
    def _():
        sum_start(2)

    sum_start(0)
    for dx in range(1, COLS):
        part_arrived(dx, 0)
    for i in (0, 1):
        sum_copy(i).wait_recv()

    @pl.when(has_extra)
    def _():
        sum_copy(2).wait_recv()

    @pl.when(jnp.logical_not(has_extra))
    def _():
        from_rows[2] = jnp.zeros((depth, WB, across), jnp.float32)

    def add_up(c, _):
        place = pl.ds(pl.multiple_of(c * CHUNK, CHUNK), CHUNK)
        gradient_out[place] = summed(0, True, c) + from_rows[0, place] + from_rows[1, place] + from_rows[2, place]
        return 0

    lax.fori_loop(0, chunks, add_up, 0)
    for which in range(2):
        for side in range(2):
            halo_sent(0, which, side)
            halo_sent(STEPS - 1, which, side)
    for i in (0, 1):
        row_copy(i).wait_send()
        sum_copy(i).wait_send()

    @pl.when(has_extra)
    def _():
        row_copy(2).wait_send()
        sum_copy(2).wait_send()

    for dx in range(1, COLS):
        for t in range(3):
            piece_copy(dx, slab_row(dx) + t).wait_send()
            part_copy(dx, first_row(col, dx) + t).wait_send()


def write_out(*refs):
    copies = [pltpu.make_async_copy(refs[i], refs[3 + i], refs[6].at[i]) for i in range(3)]
    for copy in copies:
        copy.start()
    for copy in copies:
        copy.wait()


def per_device(
    squared_courant,
    window_offset,
    field_last,
    field_after,
    adjoint_last,
    adjoint_after,
    source_place,
    source_wavelet,
    receiver_place,
    receiver_trace,
):
    _, depth, width, across = field_last.shape
    smem = pl.BlockSpec(memory_space=pltpu.SMEM)
    vmem = pl.BlockSpec(memory_space=pltpu.VMEM)
    hbm = pl.BlockSpec(memory_space=pl.ANY)
    f32 = jnp.float32
    dma = pltpu.SemaphoreType.DMA
    field, adjoint, gradient = pl.pallas_call(
        kernel,
        out_shape=(
            pltpu.VMEM((depth, width, across), f32),
            pltpu.VMEM((depth, width, across), f32),
            pltpu.VMEM((depth, WB, across), f32),
        ),
        in_specs=[smem] * 3 + [hbm] * 7,
        out_specs=(vmem, vmem, vmem),
        scratch_shapes=[
            *[pltpu.VMEM((depth + 2 * HALO, width, across), f32)] * 4,
            pltpu.VMEM((SPAN + 1, depth, WB, across), f32),
            pltpu.VMEM((2, depth, width, across), f32),
            pltpu.VMEM((depth, width, across), f32),
            pltpu.VMEM((depth, width, across), f32),
            pltpu.VMEM((SPAN + 4, depth, WB, across), f32),
            pltpu.VMEM((SPAN, depth, WB, across), f32),
            pltpu.VMEM((COLS - 1, 4, depth, WB, across), f32),
            pltpu.VMEM((3, depth, WB, across), f32),
            pltpu.VMEM((3, depth, WB, across), f32),
            pltpu.VMEM((3, 1, across), jnp.int32),
            pltpu.VMEM((STEPS, across), f32),
            pltpu.VMEM((width, across), f32),
            pltpu.VMEM((depth * width, across), jnp.bfloat16),
            pltpu.VMEM((STEPS, across, 2 * across), jnp.bfloat16),
            dma((7,)),
            dma((STEPS, 2, 2)),
            dma((STEPS, 2, 2)),
            dma((3,)),
            dma((3,)),
            dma((COLS - 1, 3)),
            dma((SPAN,)),
            dma((COLS - 1, 3)),
            dma((COLS - 1, 3)),
            dma((3,)),
            dma((3,)),
        ],
        compiler_params=pltpu.CompilerParams(
            collective_id=0, has_side_effects=True, vmem_limit_bytes=56 * 1024 * 1024
        ),
        name="inversion",
    )(
        window_offset,
        source_place[0],
        source_wavelet[0],
        receiver_place.transpose(1, 0, 2),
        receiver_trace[0],
        squared_courant,
        field_last[0],
        field_after[0],
        adjoint_last[0],
        adjoint_after[0],
    )
    results = pl.pallas_call(
        write_out,
        out_shape=tuple(jax.ShapeDtypeStruct(x.shape, f32) for x in (field, adjoint, gradient)),
        in_specs=[vmem] * 3,
        out_specs=(hbm, hbm, hbm),
        scratch_shapes=[dma((3,))],
        compiler_params=pltpu.CompilerParams(vmem_limit_bytes=4 * 1024 * 1024),
        name="write_out",
    )(field, adjoint, gradient)
    return results[0][None], results[1][None], results[2]


def solution(mesh):
    placed = (
        P("gz", "shot", None),
        P("shot"),
        P("shot", "gz", None, None),
        P("shot", "gz", None, None),
        P("shot", "gz", None, None),
        P("shot", "gz", None, None),
        P("shot", None),
        P("shot", None),
        P("shot", None, None),
        P("shot", None, None),
    )
    return jax.shard_map(
        per_device,
        mesh=mesh,
        in_specs=placed,
        out_specs=(P("shot", "gz", None, None), P("shot", "gz", None, None), P("gz", "shot", None)),
        check_vma=False,
    )
```

```python
import functools
import math

import jax
import jax.numpy as jnp
from jax import lax
from jax.experimental import pallas as pl
from jax.experimental.pallas import tpu as pltpu
from jax.sharding import PartitionSpec as P

WB = 8
COLS = 4
FIRST = (0, 1, -2, -1)
SPREAD = 2
STEPS = 4
SPAN = WB + 2 * SPREAD
HALO = 4
CHUNK = 4
BLOCK = 12
PARTS = 2
SCALE = 5040.0
CENTRE = -3.0 * 14350.0
SIDE = (8064.0, -1008.0, 128.0, -9.0)
MESH = pl.DeviceIdType.MESH


def banded(rows, cols, period):
    i = lax.broadcasted_iota(jnp.int32, (rows, cols), 0)
    j = lax.broadcasted_iota(jnp.int32, (rows, cols), 1)
    gap = jnp.abs(lax.rem(i, period) - lax.rem(j, period))
    band = jnp.zeros((rows, cols), jnp.float32)
    for k in range(1, 5):
        band = jnp.where(gap == k, SIDE[k - 1], band)
    return band.astype(jnp.bfloat16)


def in_two(values):
    high = values.astype(jnp.bfloat16)
    low = (values - high.astype(jnp.float32)).astype(jnp.bfloat16)
    return high, low


def kernel(
    offset_ref,
    spot_ref,
    wavelet_ref,
    receivers_in,
    traces_in,
    courant_ref,
    field_last,
    field_after,
    adjoint_last,
    adjoint_after,
    field_out,
    adjoint_out,
    gradient_out,
    field_a,
    adjoint_a,
    field_b,
    adjoint_b,
    pieces_low,
    pieces_high,
    laps,
    model,
    imaging,
    shown,
    outgoing,
    from_row,
    sums,
    from_rows,
    receivers_ref,
    traces_ref,
    taper_ref,
    hits,
    amounts,
    load_sem,
    halo_send,
    halo_recv,
    row_send,
    row_recv,
    piece_send,
    piece_recv,
    back_send,
    back_recv,
    sum_send,
    sum_recv,
):
    fields = ((field_a, adjoint_a), (field_b, adjoint_b))
    pieces = (pieces_low, pieces_high)
    shot = lax.axis_index("shot")
    slab = lax.axis_index("gz")
    shots = lax.axis_size("shot")
    slabs = lax.axis_size("gz")
    depth, width, across = field_last.shape
    chunks = depth // CHUNK
    half = depth // PARTS
    has = (slab > 0, slab < slabs - 1)
    beside = (jnp.maximum(slab - 1, 0), jnp.minimum(slab + 1, slabs - 1))

    row, col = shot // COLS, lax.rem(shot, COLS)
    rows = shots // COLS
    has_extra = col != 1
    extra_row = jnp.where(col == 0, 3, -1)

    def in_row(dx):
        return row * COLS + lax.rem(col + dx, COLS)

    def in_column(r):
        return lax.rem(row + r + rows, rows) * COLS + col

    def first_row(source, dx):
        return (source + FIRST[dx] - lax.rem(source + dx, COLS)) // COLS

    loads = []
    for i, (buffer, which, source) in enumerate(
        ((0, 0, field_last), (0, 1, adjoint_last), (1, 0, field_after), (1, 1, adjoint_after))
    ):
        loads.append(pltpu.make_async_copy(source, fields[buffer][which].at[pl.ds(HALO, depth)], load_sem.at[i]))
    for i, (source, place) in enumerate(
        (
            (courant_ref.at[pl.ds(0, half)], pieces[0].at[SPREAD]),
            (courant_ref.at[pl.ds(half, half)], pieces[1].at[SPREAD]),
            (receivers_in, receivers_ref),
            (traces_in, traces_ref),
        )
    ):
        loads.append(pltpu.make_async_copy(source, place, load_sem.at[4 + i]))
    for copy in loads:
        copy.start()

    blank = jnp.zeros((HALO, width, across), jnp.float32)
    for side, place in ((0, 0), (1, HALO + depth)):

        @pl.when(jnp.logical_not(has[side]))
        def _():
            for buffer in range(2):
                for which in range(2):
                    fields[buffer][which][pl.ds(place, HALO)] = blank

    barrier = pltpu.get_barrier_semaphore()
    for dx in range(1, COLS):
        pl.semaphore_signal(barrier, inc=1, device_id={"shot": in_row(dx)}, device_id_type=MESH)
    for r in (-3, -1, 1, 3):
        pl.semaphore_signal(barrier, inc=1, device_id={"shot": in_column(r)}, device_id_type=MESH)
    for side in range(2):

        @pl.when(has[side])
        def _():
            pl.semaphore_signal(barrier, inc=1, device_id={"gz": beside[side]}, device_id_type=MESH)

    beside_count = jnp.where(has[0], 1, 0) + jnp.where(has[1], 1, 0)
    pl.semaphore_wait(barrier, COLS - 1 + 4 + beside_count)

    def halo(turn, which, side):
        place = HALO if side == 0 else depth
        landing = HALO + depth if side == 0 else 0
        if turn == 0:
            source = (field_last, adjoint_last)[which].at[pl.ds(place - HALO, HALO)]
        else:
            source = fields[turn % 2][which].at[pl.ds(place, HALO)]
        return pltpu.make_async_remote_copy(
            src_ref=source,
            dst_ref=fields[turn % 2][which].at[pl.ds(landing, HALO)],
            send_sem=halo_send.at[turn, which, side],
            recv_sem=halo_recv.at[turn, which, side],
            device_id={"gz": beside[side]},
            device_id_type=MESH,
        )

    def halo_start(turn, which, side):
        @pl.when(has[side])
        def _():
            halo(turn, which, side).start()

    def halo_arrived(turn, which, side):
        @pl.when(has[side])
        def _():
            halo(turn, which, 1 - side).wait_recv()

    def halo_sent(turn, which, side):
        @pl.when(has[side])
        def _():
            halo(turn, which, side).wait_send()

    def row_copy(i, h):
        return pltpu.make_async_remote_copy(
            src_ref=pieces[h].at[SPREAD + COLS] if i == 1 else courant_ref.at[pl.ds(h * half, half)],
            dst_ref=pieces[h].at[(SPREAD + COLS, SPREAD + 2 * COLS, SPAN)[i]],
            send_sem=row_send.at[i, h],
            recv_sem=row_recv.at[i, h],
            device_id={"shot": in_column((-1, -1, -extra_row)[i])},
            device_id_type=MESH,
        )

    def piece_copy(dx, r, h):
        target = lax.rem(col + dx, COLS)
        slot = COLS * r + col - target + SPREAD
        held = jnp.where((r >= 0) & (r <= 2), SPREAD + COLS * r, SPAN)
        return pltpu.make_async_remote_copy(
            src_ref=pieces[h].at[held],
            dst_ref=pieces[h].at[slot],
            send_sem=piece_send.at[dx - 1, r - slab_row(dx), h],
            recv_sem=piece_recv.at[slot, h],
            device_id={"shot": in_row(dx)},
            device_id_type=MESH,
        )

    def slab_row(dx):
        return first_row(lax.rem(col + dx, COLS), COLS - dx)

    def pieces_arrived(h):
        for j in range(SPAN):
            if j % COLS != SPREAD:
                pltpu.make_async_copy(pieces[h].at[j], pieces[h].at[j], piece_recv.at[j, h]).wait()

    def part_copy(dx, r, h):
        target = lax.rem(col + dx, COLS)
        at = r - first_row(col, dx)
        return pltpu.make_async_remote_copy(
            src_ref=outgoing.at[COLS * r + target - col + SPREAD, pl.ds(h * half, half)],
            dst_ref=from_row.at[dx - 1, at, pl.ds(h * half, half)],
            send_sem=back_send.at[dx - 1, at, h],
            recv_sem=back_recv.at[dx - 1, at, h],
            device_id={"shot": in_row(dx)},
            device_id_type=MESH,
        )

    def parts_start(r, h):
        for dx in (1, 3, 2):
            first = first_row(col, dx)

            @pl.when((r >= first) & (r <= first + 2))
            def _():
                part_copy(dx, r, h).start()

    def source_row(dx):
        return first_row(lax.rem(col - dx + COLS, COLS), dx)

    def parts_arrived(r, h):
        for dx in range(1, COLS):
            first = source_row(dx)

            @pl.when((r >= first) & (r <= first + 2))
            def _():
                place = from_row.at[dx - 1, r - first, pl.ds(h * half, half)]
                pltpu.make_async_copy(place, place, back_recv.at[dx - 1, r - first, h]).wait()

    def summed(r, own, place):
        total = outgoing[SPREAD + COLS * r, place] if own else jnp.zeros((CHUNK, WB, across), jnp.float32)
        for dx in range(1, COLS):
            at = r - source_row(dx)
            total = total + from_row[dx - 1, jnp.where((at >= 0) & (at <= 2), at, 3), place]
        return total

    def sum_copy(i, h):
        return pltpu.make_async_remote_copy(
            src_ref=sums.at[i, pl.ds(h * half, half)],
            dst_ref=from_rows.at[i, pl.ds(h * half, half)],
            send_sem=sum_send.at[i, h],
            recv_sem=sum_recv.at[i, h],
            device_id={"shot": in_column((1, 1, extra_row)[i])},
            device_id_type=MESH,
        )

    def over_half(h, body):
        def turn(c, _):
            body(pl.ds(pl.multiple_of(c * CHUNK, CHUNK), CHUNK))
            return 0

        count = half // CHUNK
        lax.fori_loop(h * count, (h + 1) * count, turn, 0)

    def sum_start(i, h):
        r = (1, 2, extra_row)[i]
        parts_arrived(r, h)
        if i == 0:
            sum_copy(1, h).wait_recv()

        def body(place):
            total = summed(r, i < 2, place)
            sums[i, place] = total + from_rows[1, place] if i == 0 else total

        over_half(h, body)
        sum_copy(i, h).start()

    def rows_start(h):
        row_copy(0, h).start()

        @pl.when(has_extra)
        def _():
            row_copy(2, h).start()

    rows_start(0)
    for h in range(PARTS):
        loads[4 + h].wait()
        for dx in (1, 3, 2):

            @pl.when(slab_row(dx) <= 0)
            def _():
                piece_copy(dx, 0, h).start()

    offset = offset_ref[0]
    for copy in loads[6:]:
        copy.wait()
    by_y = banded(2 * across, across, across)
    by_x = banded(width, 2 * width, width)
    cell = lax.broadcasted_iota(jnp.int32, (width * CHUNK, across), 0)
    place = (receivers_ref[0] - slab * depth) * width + receivers_ref[1]

    def mark(c, _):
        start = pl.multiple_of(c * CHUNK * width, CHUNK * width)
        hits[pl.ds(start, CHUNK * width), :] = jnp.where(cell + start == place, 1.0, 0.0).astype(jnp.bfloat16)
        return 0

    lax.fori_loop(0, chunks, mark, 0)
    along = lax.broadcasted_iota(jnp.int32, (across, across), 0) == receivers_ref[2]
    for step in range(STEPS):
        high, low = in_two(jnp.where(along, traces_ref[step : step + 1, :], 0.0))
        amounts[step, :, 0:across] = high
        amounts[step, :, across : 2 * across] = low
    across_x = lax.broadcasted_iota(jnp.int32, (width, across), 0).astype(jnp.float32)
    taper_ref[...] = jnp.sin((across_x + 0.5) * (math.pi / width)) ** 2 * (1.0 / SCALE)
    spot = jnp.where(
        (lax.broadcasted_iota(jnp.int32, (width, across), 0) == spot_ref[1])
        & (lax.broadcasted_iota(jnp.int32, (width, across), 1) == spot_ref[2]),
        1.0,
        0.0,
    )
    spot_depth = spot_ref[0] - slab * depth
    shown[pl.ds(0, 4)] = jnp.zeros((4, depth, WB, across), jnp.float32)
    shown[pl.ds(12, 4)] = jnp.zeros((4, depth, WB, across), jnp.float32)

    def flat(high, low, planes):
        rows = planes * width
        left = jnp.concatenate([high.reshape(rows, across), low.reshape(rows, across)], axis=1)
        in_y = jnp.dot(left, by_y, preferred_element_type=jnp.float32)
        right = jnp.concatenate(
            [jnp.concatenate([part[c] for c in range(planes)], axis=1) for part in (high, low)], axis=0
        )
        in_x = jnp.dot(by_x, right, preferred_element_type=jnp.float32)
        return in_y, in_x

    def spans(starts, planes):
        return [(z0, i * planes) for i, z0 in enumerate(starts)]

    def injected(step, starts, planes):
        found = []
        for z0 in starts:
            found.append(hits[pl.ds(pl.multiple_of(z0 * width, CHUNK * width), planes * width), :])
        found = jnp.concatenate(found, axis=0)
        return lax.dot_general(
            jnp.concatenate([found, found], axis=1),
            amounts[step],
            (((1,), (1,)), ((), ())),
            preferred_element_type=jnp.float32,
        )

    def laplace(now, starts, planes, use):
        high, low = in_two(jnp.concatenate([now[pl.ds(z0 + HALO, planes)] for z0 in starts], axis=0))
        in_y, in_x = flat(high, low, planes * len(starts))
        for s in range(width // WB):
            tile = pl.ds(s * WB, WB)
            for z0, first in spans(starts, planes):
                line = [now[z0 + c, tile] for c in range(planes + 2 * HALO)]
                for c in range(planes):
                    at = first + c
                    centre = line[c + HALO]
                    total = CENTRE * centre + in_y[at * width + s * WB : at * width + (s + 1) * WB]
                    total = total + in_x[s * WB : (s + 1) * WB, at * across : (at + 1) * across]
                    for k in range(1, 5):
                        total = total + SIDE[k - 1] * (line[c + HALO + k] + line[c + HALO - k])
                    use(z0 + c, at, s, tile, centre, total)

    def see(step, z, s, tile, lap):
        seen = fields[step % 2][1][z + HALO, tile] * lap
        if step > 0:
            seen = imaging[z, tile] + seen
        if step < STEPS - 1:
            imaging[z, tile] = seen
        else:
            shown[4 + s, z] = taper_ref[tile] * seen

    def advance(step, which, z, tile, centre, lap, extra):
        later = fields[1 - step % 2][which]
        new = 2.0 * centre - later[z + HALO, tile] + model[z, tile] * lap + extra
        if step < STEPS - 1:
            later[z + HALO, tile] = new
        else:
            (field_out, adjoint_out)[which][z, tile] = new

    def extras(step, which, starts, planes):
        if which == 0:
            return lambda z, at, s, tile: spot[s * WB : (s + 1) * WB] * jnp.where(
                z == spot_depth, wavelet_ref[step], 0.0
            )
        added = injected(step, starts, planes)
        return lambda z, at, s, tile: added[at * width + s * WB : at * width + (s + 1) * WB]

    def first_part(which, starts, planes):
        def use(z, at, s, tile, centre, lap):
            laps[which, z, tile] = lap
            if which == 0:
                see(0, z, s, tile, lap)

        laplace(fields[0][which], starts, planes, use)

    def second_part(which, starts, planes):
        extra = extras(0, which, starts, planes)
        for s in range(width // WB):
            tile = pl.ds(s * WB, WB)
            for z0, first in spans(starts, planes):
                for c in range(planes):
                    z = z0 + c
                    centre = fields[0][which][z + HALO, tile]
                    advance(0, which, z, tile, centre, laps[which, z, tile], extra(z, first + c, s, tile))

    def whole(step, which, starts, planes):
        extra = extras(step, which, starts, planes)

        def use(z, at, s, tile, centre, lap):
            if which == 0:
                see(step, z, s, tile, lap)
            advance(step, which, z, tile, centre, lap, extra(z, at, s, tile))

        laplace(fields[step % 2][which], starts, planes, use)

    def inner(body, first=0, last=(depth - 2 * HALO) // BLOCK):
        def turn(c, _):
            body([pl.multiple_of(c * BLOCK + HALO, CHUNK)], BLOCK)
            return 0

        lax.fori_loop(first, last, turn, 0)

    def pass_on_near(h):
        row_copy(0, h).wait_recv()
        row_copy(1, h).start()
        for dx in (1, 3, 2):
            piece_copy(dx, 1, h).start()

        @pl.when(has_extra)
        def _():
            row_copy(2, h).wait_recv()

        for dx in range(1, COLS):
            first = slab_row(dx)

            @pl.when(first != 0)
            def _():
                piece_copy(dx, jnp.where(first < 0, -1, 3), h).start()

    def pass_on_later(h):
        row_copy(1, h).wait_recv()
        for dx in (1, 3, 2):

            @pl.when(slab_row(dx) >= 0)
            def _():
                piece_copy(dx, 2, h).start()

    def build_model(h):
        pieces_arrived(h)
        for s in range(WB):
            model[pl.ds(h * half, half), pl.ds(s * WB, WB), :] = pieces[h][offset + SPREAD + s] * (1.0 / SCALE)

    ends = (0, depth - CHUNK)
    for copy in loads[:2]:
        copy.wait()
    inner(functools.partial(first_part, 0))
    row_copy(0, 0).wait_send()
    rows_start(1)
    inner(functools.partial(first_part, 1))
    for h in range(PARTS):
        pass_on_near(h)
    for h in range(PARTS):
        pass_on_later(h)
    for which in range(2):
        for side in range(2):
            halo_start(0, which, side)
    for copy in loads[2:4]:
        copy.wait()
    build_model(0)
    for which in range(2):
        inner(functools.partial(second_part, which), 0, 1)
    for which in range(2):
        for side in range(2):
            halo_arrived(0, which, side)
        first_part(which, ends, CHUNK)
    build_model(1)
    for which in range(2):
        second_part(which, ends, CHUNK)
        for side in range(2):
            halo_start(1, which, side)
    for which in range(2):
        inner(functools.partial(second_part, which), 1)

    def image_out(h):
        place = pl.ds(h * half, half)
        for j in range(SPAN):
            outgoing[j, place] = shown[j + 2 - offset, place]
        for r in (2, -1, 3):
            parts_start(r, h)

    from_row[:, 3] = jnp.zeros((COLS - 1, depth, WB, across), jnp.float32)
    for step in range(1, STEPS):
        for which in range(2):
            body = functools.partial(whole, step, which)
            for side in range(2):
                halo_arrived(step, which, side)
                if step > 1:
                    halo_sent(step - 1, which, side)
            body(ends, CHUNK)
            if step < STEPS - 1:
                for side in range(2):
                    halo_start(step + 1, which, side)
                inner(body)
            elif which == 0:
                inner(body, 0, 1)
                image_out(0)
                inner(body, 1)
                image_out(1)
            else:
                for h in range(PARTS):
                    parts_start(1, h)
                inner(body)
    for h in range(PARTS):
        sum_start(1, h)

        @pl.when(has_extra)
        def _():
            sum_start(2, h)

        parts_start(0, h)
    for h in range(PARTS):
        sum_start(0, h)

    @pl.when(jnp.logical_not(has_extra))
    def _():
        from_rows[2] = jnp.zeros((depth, WB, across), jnp.float32)

    for h in range(PARTS):
        parts_arrived(0, h)
        sum_copy(0, h).wait_recv()

        @pl.when(has_extra)
        def _():
            sum_copy(2, h).wait_recv()

        def add_up(place):
            gradient_out[place] = summed(0, True, place) + from_rows[0, place] + from_rows[2, place]

        over_half(h, add_up)
    for which in range(2):
        for side in range(2):
            halo_sent(0, which, side)
            halo_sent(STEPS - 1, which, side)
    for h in range(PARTS):
        if h > 0:
            row_copy(0, h).wait_send()
        row_copy(1, h).wait_send()
        for i in (0, 1):
            sum_copy(i, h).wait_send()

        @pl.when(has_extra)
        def _():
            row_copy(2, h).wait_send()
            sum_copy(2, h).wait_send()

        for dx in range(1, COLS):
            for t in range(3):
                piece_copy(dx, slab_row(dx) + t, h).wait_send()
                part_copy(dx, first_row(col, dx) + t, h).wait_send()


def write_out(*refs):
    copies = [pltpu.make_async_copy(refs[i], refs[3 + i], refs[6].at[i]) for i in range(3)]
    for copy in copies:
        copy.start()
    for copy in copies:
        copy.wait()


def per_device(
    squared_courant,
    window_offset,
    field_last,
    field_after,
    adjoint_last,
    adjoint_after,
    source_place,
    source_wavelet,
    receiver_place,
    receiver_trace,
):
    _, depth, width, across = field_last.shape
    smem = pl.BlockSpec(memory_space=pltpu.SMEM)
    vmem = pl.BlockSpec(memory_space=pltpu.VMEM)
    hbm = pl.BlockSpec(memory_space=pl.ANY)
    f32 = jnp.float32
    dma = pltpu.SemaphoreType.DMA
    field, adjoint, gradient = pl.pallas_call(
        kernel,
        out_shape=(
            pltpu.VMEM((depth, width, across), f32),
            pltpu.VMEM((depth, width, across), f32),
            pltpu.VMEM((depth, WB, across), f32),
        ),
        in_specs=[smem] * 3 + [hbm] * 7,
        out_specs=(vmem, vmem, vmem),
        scratch_shapes=[
            *[pltpu.VMEM((depth + 2 * HALO, width, across), f32)] * 4,
            *[pltpu.VMEM((SPAN + 1, depth // PARTS, WB, across), f32)] * PARTS,
            pltpu.VMEM((2, depth, width, across), f32),
            pltpu.VMEM((depth, width, across), f32),
            pltpu.VMEM((depth, width, across), f32),
            pltpu.VMEM((SPAN + 4, depth, WB, across), f32),
            pltpu.VMEM((SPAN, depth, WB, across), f32),
            pltpu.VMEM((COLS - 1, 4, depth, WB, across), f32),
            pltpu.VMEM((3, depth, WB, across), f32),
            pltpu.VMEM((3, depth, WB, across), f32),
            pltpu.VMEM((3, 1, across), jnp.int32),
            pltpu.VMEM((STEPS, across), f32),
            pltpu.VMEM((width, across), f32),
            pltpu.VMEM((depth * width, across), jnp.bfloat16),
            pltpu.VMEM((STEPS, across, 2 * across), jnp.bfloat16),
            dma((8,)),
            dma((STEPS, 2, 2)),
            dma((STEPS, 2, 2)),
            dma((3, PARTS)),
            dma((3, PARTS)),
            dma((COLS - 1, 3, PARTS)),
            dma((SPAN, PARTS)),
            dma((COLS - 1, 3, PARTS)),
            dma((COLS - 1, 3, PARTS)),
            dma((3, PARTS)),
            dma((3, PARTS)),
        ],
        compiler_params=pltpu.CompilerParams(
            collective_id=0, has_side_effects=True, vmem_limit_bytes=56 * 1024 * 1024
        ),
        name="inversion",
    )(
        window_offset,
        source_place[0],
        source_wavelet[0],
        receiver_place.transpose(1, 0, 2),
        receiver_trace[0],
        squared_courant,
        field_last[0],
        field_after[0],
        adjoint_last[0],
        adjoint_after[0],
    )
    results = pl.pallas_call(
        write_out,
        out_shape=tuple(jax.ShapeDtypeStruct(x.shape, f32) for x in (field, adjoint, gradient)),
        in_specs=[vmem] * 3,
        out_specs=(hbm, hbm, hbm),
        scratch_shapes=[dma((3,))],
        compiler_params=pltpu.CompilerParams(vmem_limit_bytes=4 * 1024 * 1024),
        name="write_out",
    )(field, adjoint, gradient)
    return results[0][None], results[1][None], results[2]


def solution(mesh):
    placed = (
        P("gz", "shot", None),
        P("shot"),
        P("shot", "gz", None, None),
        P("shot", "gz", None, None),
        P("shot", "gz", None, None),
        P("shot", "gz", None, None),
        P("shot", None),
        P("shot", None),
        P("shot", None, None),
        P("shot", None, None),
    )
    return jax.shard_map(
        per_device,
        mesh=mesh,
        in_specs=placed,
        out_specs=(P("shot", "gz", None, None), P("shot", "gz", None, None), P("gz", "shot", None)),
        check_vma=False,
    )
```

```python
import functools
import math

import jax
import jax.numpy as jnp
from jax import lax
from jax.experimental import pallas as pl
from jax.experimental.pallas import tpu as pltpu
from jax.sharding import PartitionSpec as P

WB = 8
COLS = 4
FIRST = (0, 1, -2, -1)
SPREAD = 2
STEPS = 4
SPAN = WB + 2 * SPREAD
FAR = WB + SPREAD - 1
HALO = 4
CHUNK = 4
BLOCK = 12
PARTS = 2
SCALE = 5040.0
CENTRE = -3.0 * 14350.0
SIDE = (8064.0, -1008.0, 128.0, -9.0)
MESH = pl.DeviceIdType.MESH


def banded(rows, cols, period):
    i = lax.broadcasted_iota(jnp.int32, (rows, cols), 0)
    j = lax.broadcasted_iota(jnp.int32, (rows, cols), 1)
    gap = jnp.abs(lax.rem(i, period) - lax.rem(j, period))
    band = jnp.zeros((rows, cols), jnp.float32)
    for k in range(1, 5):
        band = jnp.where(gap == k, SIDE[k - 1], band)
    return band.astype(jnp.bfloat16)


def in_two(values):
    high = values.astype(jnp.bfloat16)
    low = (values - high.astype(jnp.float32)).astype(jnp.bfloat16)
    return high, low


def kernel(
    offset_ref,
    spot_ref,
    wavelet_ref,
    receivers_in,
    traces_in,
    courant_ref,
    field_last,
    field_after,
    adjoint_last,
    adjoint_after,
    field_out,
    adjoint_out,
    gradient_out,
    field_a,
    adjoint_a,
    field_b,
    adjoint_b,
    pieces_low,
    pieces_high,
    laps,
    model,
    imaging,
    shown,
    outgoing,
    from_row,
    sums,
    from_rows,
    receivers_ref,
    traces_ref,
    taper_ref,
    hits,
    amounts,
    load_sem,
    halo_send,
    halo_recv,
    row_send,
    row_recv,
    piece_send,
    piece_recv,
    back_send,
    back_recv,
    sum_send,
    sum_recv,
):
    fields = ((field_a, adjoint_a), (field_b, adjoint_b))
    pieces = (pieces_low, pieces_high)
    shot = lax.axis_index("shot")
    slab = lax.axis_index("gz")
    shots = lax.axis_size("shot")
    slabs = lax.axis_size("gz")
    depth, width, across = field_last.shape
    chunks = depth // CHUNK
    half = depth // PARTS
    has = (slab > 0, slab < slabs - 1)
    beside = (jnp.maximum(slab - 1, 0), jnp.minimum(slab + 1, slabs - 1))

    row, col = shot // COLS, lax.rem(shot, COLS)
    rows = shots // COLS
    has_extra = col > 1
    is_far = (col == 0) | (col == COLS - 1)
    far_shot = lax.rem(jnp.where(col == 0, shot - FAR, shot + FAR) + shots, shots)

    def in_row(dx):
        return row * COLS + lax.rem(col + dx, COLS)

    def in_column(r):
        return lax.rem(row + r + rows, rows) * COLS + col

    def first_row(source, dx):
        return (source + FIRST[dx] - lax.rem(source + dx, COLS)) // COLS

    loads = []
    for i, (buffer, which, source) in enumerate(
        ((0, 0, field_last), (0, 1, adjoint_last), (1, 0, field_after), (1, 1, adjoint_after))
    ):
        loads.append(pltpu.make_async_copy(source, fields[buffer][which].at[pl.ds(HALO, depth)], load_sem.at[i]))
    for i, (source, place) in enumerate(
        (
            (courant_ref.at[pl.ds(0, half)], pieces[0].at[SPREAD]),
            (courant_ref.at[pl.ds(half, half)], pieces[1].at[SPREAD]),
            (receivers_in, receivers_ref),
            (traces_in, traces_ref),
        )
    ):
        loads.append(pltpu.make_async_copy(source, place, load_sem.at[4 + i]))
    for copy in loads:
        copy.start()

    blank = jnp.zeros((HALO, width, across), jnp.float32)
    for side, place in ((0, 0), (1, HALO + depth)):

        @pl.when(jnp.logical_not(has[side]))
        def _():
            for buffer in range(2):
                for which in range(2):
                    fields[buffer][which][pl.ds(place, HALO)] = blank

    barrier = pltpu.get_barrier_semaphore()
    for dx in range(1, COLS):
        pl.semaphore_signal(barrier, inc=1, device_id={"shot": in_row(dx)}, device_id_type=MESH)
    for r in (-1, 1):
        pl.semaphore_signal(barrier, inc=1, device_id={"shot": in_column(r)}, device_id_type=MESH)

    @pl.when(is_far)
    def _():
        pl.semaphore_signal(barrier, inc=1, device_id={"shot": far_shot}, device_id_type=MESH)

    for side in range(2):

        @pl.when(has[side])
        def _():
            pl.semaphore_signal(barrier, inc=1, device_id={"gz": beside[side]}, device_id_type=MESH)

    beside_count = jnp.where(has[0], 1, 0) + jnp.where(has[1], 1, 0)
    pl.semaphore_wait(barrier, COLS - 1 + 2 + jnp.where(is_far, 1, 0) + beside_count)

    def halo(turn, which, side):
        place = HALO if side == 0 else depth
        landing = HALO + depth if side == 0 else 0
        if turn == 0:
            source = (field_last, adjoint_last)[which].at[pl.ds(place - HALO, HALO)]
        else:
            source = fields[turn % 2][which].at[pl.ds(place, HALO)]
        return pltpu.make_async_remote_copy(
            src_ref=source,
            dst_ref=fields[turn % 2][which].at[pl.ds(landing, HALO)],
            send_sem=halo_send.at[turn, which, side],
            recv_sem=halo_recv.at[turn, which, side],
            device_id={"gz": beside[side]},
            device_id_type=MESH,
        )

    def halo_start(turn, which, side):
        @pl.when(has[side])
        def _():
            halo(turn, which, side).start()

    def halo_arrived(turn, which, side):
        @pl.when(has[side])
        def _():
            halo(turn, which, 1 - side).wait_recv()

    def halo_sent(turn, which, side):
        @pl.when(has[side])
        def _():
            halo(turn, which, side).wait_send()

    def row_copy(i, h):
        return pltpu.make_async_remote_copy(
            src_ref=pieces[h].at[SPREAD + COLS] if i == 1 else courant_ref.at[pl.ds(h * half, half)],
            dst_ref=pieces[h].at[(SPREAD + COLS, SPREAD + 2 * COLS, SPAN)[i]],
            send_sem=row_send.at[i, h],
            recv_sem=row_recv.at[i, h],
            device_id={"shot": in_column((-1, -1, 1)[i])},
            device_id_type=MESH,
        )

    def piece_copy(dx, r, h):
        target = lax.rem(col + dx, COLS)
        slot = COLS * r + col - target + SPREAD
        held = jnp.where(r >= 0, jnp.minimum(SPREAD + COLS * r, SPAN), SPAN)
        return pltpu.make_async_remote_copy(
            src_ref=pieces[h].at[held],
            dst_ref=pieces[h].at[slot],
            send_sem=piece_send.at[dx - 1, r - slab_row(dx), h],
            recv_sem=piece_recv.at[slot, h],
            device_id={"shot": in_row(dx)},
            device_id_type=MESH,
        )

    def far_copy(h):
        return pltpu.make_async_remote_copy(
            src_ref=courant_ref.at[pl.ds(h * half, half)],
            dst_ref=pieces[h].at[SPAN - 1],
            send_sem=piece_send.at[COLS - 2, 2, h],
            recv_sem=piece_recv.at[SPAN - 1, h],
            device_id={"shot": far_shot},
            device_id_type=MESH,
        )

    def far_part(h):
        return pltpu.make_async_remote_copy(
            src_ref=outgoing.at[SPAN - 1, pl.ds(h * half, half)],
            dst_ref=from_rows.at[2, pl.ds(h * half, half)],
            send_sem=back_send.at[0, 2, h],
            recv_sem=sum_recv.at[2, h],
            device_id={"shot": far_shot},
            device_id_type=MESH,
        )

    def slab_row(dx):
        return first_row(lax.rem(col + dx, COLS), COLS - dx)

    def pieces_arrived(h):
        for j in range(SPAN):
            if j % COLS != SPREAD:
                pltpu.make_async_copy(pieces[h].at[j], pieces[h].at[j], piece_recv.at[j, h]).wait()

    def part_copy(dx, r, h):
        target = lax.rem(col + dx, COLS)
        at = r - first_row(col, dx)
        return pltpu.make_async_remote_copy(
            src_ref=outgoing.at[COLS * r + target - col + SPREAD, pl.ds(h * half, half)],
            dst_ref=from_row.at[dx - 1, at, pl.ds(h * half, half)],
            send_sem=back_send.at[dx - 1, at, h],
            recv_sem=back_recv.at[dx - 1, at, h],
            device_id={"shot": in_row(dx)},
            device_id_type=MESH,
        )

    def parts_start(r, h):
        for dx in (1, 3, 2):
            first = first_row(col, dx)

            @pl.when((r >= first) & (r <= first + 2))
            def _():
                part_copy(dx, r, h).start()

    def source_row(dx):
        return first_row(lax.rem(col - dx + COLS, COLS), dx)

    def parts_arrived(r, h):
        for dx in range(1, COLS):
            first = source_row(dx)

            @pl.when((r >= first) & (r <= first + 2))
            def _():
                place = from_row.at[dx - 1, r - first, pl.ds(h * half, half)]
                pltpu.make_async_copy(place, place, back_recv.at[dx - 1, r - first, h]).wait()

    def summed(r, own, place):
        total = outgoing[SPREAD + COLS * r, place] if own else jnp.zeros((CHUNK, WB, across), jnp.float32)
        for dx in range(1, COLS):
            at = r - source_row(dx)
            total = total + from_row[dx - 1, jnp.where((at >= 0) & (at <= 2), at, 3), place]
        return total

    def sum_copy(i, h):
        return pltpu.make_async_remote_copy(
            src_ref=sums.at[i, pl.ds(h * half, half)],
            dst_ref=from_rows.at[i, pl.ds(h * half, half)],
            send_sem=sum_send.at[i, h],
            recv_sem=sum_recv.at[i, h],
            device_id={"shot": in_column((1, 1, -1)[i])},
            device_id_type=MESH,
        )

    def over_half(h, body):
        def turn(c, _):
            body(pl.ds(pl.multiple_of(c * CHUNK, CHUNK), CHUNK))
            return 0

        count = half // CHUNK
        lax.fori_loop(h * count, (h + 1) * count, turn, 0)

    def sum_start(i, h):
        r = (1, 2, -1)[i]
        parts_arrived(r, h)
        if i == 0:
            sum_copy(1, h).wait_recv()

        def body(place):
            total = summed(r, i < 2, place)
            sums[i, place] = total + from_rows[1, place] if i == 0 else total

        over_half(h, body)
        sum_copy(i, h).start()

    def rows_start(h):
        row_copy(0, h).start()

        @pl.when(has_extra)
        def _():
            row_copy(2, h).start()

    rows_start(0)
    for h in range(PARTS):
        loads[4 + h].wait()
        for dx in (1, 3, 2):

            @pl.when(slab_row(dx) <= 0)
            def _():
                piece_copy(dx, 0, h).start()

        @pl.when(col == 0)
        def _():
            far_copy(h).start()

    offset = offset_ref[0]
    for copy in loads[6:]:
        copy.wait()
    by_y = banded(2 * across, across, across)
    by_x = banded(width, 2 * width, width)
    cell = lax.broadcasted_iota(jnp.int32, (width * CHUNK, across), 0)
    place = (receivers_ref[0] - slab * depth) * width + receivers_ref[1]

    def mark(c, _):
        start = pl.multiple_of(c * CHUNK * width, CHUNK * width)
        hits[pl.ds(start, CHUNK * width), :] = jnp.where(cell + start == place, 1.0, 0.0).astype(jnp.bfloat16)
        return 0

    lax.fori_loop(0, chunks, mark, 0)
    along = lax.broadcasted_iota(jnp.int32, (across, across), 0) == receivers_ref[2]
    for step in range(STEPS):
        high, low = in_two(jnp.where(along, traces_ref[step : step + 1, :], 0.0))
        amounts[step, :, 0:across] = high
        amounts[step, :, across : 2 * across] = low
    across_x = lax.broadcasted_iota(jnp.int32, (width, across), 0).astype(jnp.float32)
    taper_ref[...] = jnp.sin((across_x + 0.5) * (math.pi / width)) ** 2 * (1.0 / SCALE)
    spot = jnp.where(
        (lax.broadcasted_iota(jnp.int32, (width, across), 0) == spot_ref[1])
        & (lax.broadcasted_iota(jnp.int32, (width, across), 1) == spot_ref[2]),
        1.0,
        0.0,
    )
    spot_depth = spot_ref[0] - slab * depth
    shown[pl.ds(0, 4)] = jnp.zeros((4, depth, WB, across), jnp.float32)
    shown[pl.ds(12, 4)] = jnp.zeros((4, depth, WB, across), jnp.float32)

    def flat(high, low, planes):
        rows = planes * width
        left = jnp.concatenate([high.reshape(rows, across), low.reshape(rows, across)], axis=1)
        in_y = jnp.dot(left, by_y, preferred_element_type=jnp.float32)
        right = jnp.concatenate(
            [jnp.concatenate([part[c] for c in range(planes)], axis=1) for part in (high, low)], axis=0
        )
        in_x = jnp.dot(by_x, right, preferred_element_type=jnp.float32)
        return in_y, in_x

    def spans(starts, planes):
        return [(z0, i * planes) for i, z0 in enumerate(starts)]

    def injected(step, starts, planes):
        found = []
        for z0 in starts:
            found.append(hits[pl.ds(pl.multiple_of(z0 * width, CHUNK * width), planes * width), :])
        found = jnp.concatenate(found, axis=0)
        return lax.dot_general(
            jnp.concatenate([found, found], axis=1),
            amounts[step],
            (((1,), (1,)), ((), ())),
            preferred_element_type=jnp.float32,
        )

    def laplace(now, starts, planes, use):
        high, low = in_two(jnp.concatenate([now[pl.ds(z0 + HALO, planes)] for z0 in starts], axis=0))
        in_y, in_x = flat(high, low, planes * len(starts))
        for s in range(width // WB):
            tile = pl.ds(s * WB, WB)
            for z0, first in spans(starts, planes):
                line = [now[z0 + c, tile] for c in range(planes + 2 * HALO)]
                for c in range(planes):
                    at = first + c
                    centre = line[c + HALO]
                    total = CENTRE * centre + in_y[at * width + s * WB : at * width + (s + 1) * WB]
                    total = total + in_x[s * WB : (s + 1) * WB, at * across : (at + 1) * across]
                    for k in range(1, 5):
                        total = total + SIDE[k - 1] * (line[c + HALO + k] + line[c + HALO - k])
                    use(z0 + c, at, s, tile, centre, total)

    def see(step, z, s, tile, lap):
        seen = fields[step % 2][1][z + HALO, tile] * lap
        if step > 0:
            seen = imaging[z, tile] + seen
        if step < STEPS - 1:
            imaging[z, tile] = seen
        else:
            shown[4 + s, z] = taper_ref[tile] * seen

    def advance(step, which, z, tile, centre, lap, extra):
        later = fields[1 - step % 2][which]
        new = 2.0 * centre - later[z + HALO, tile] + model[z, tile] * lap + extra
        if step < STEPS - 1:
            later[z + HALO, tile] = new
        else:
            (field_out, adjoint_out)[which][z, tile] = new

    def extras(step, which, starts, planes):
        if which == 0:
            return lambda z, at, s, tile: spot[s * WB : (s + 1) * WB] * jnp.where(
                z == spot_depth, wavelet_ref[step], 0.0
            )
        added = injected(step, starts, planes)
        return lambda z, at, s, tile: added[at * width + s * WB : at * width + (s + 1) * WB]

    def first_part(which, starts, planes):
        def use(z, at, s, tile, centre, lap):
            laps[which, z, tile] = lap
            if which == 0:
                see(0, z, s, tile, lap)

        laplace(fields[0][which], starts, planes, use)

    def second_part(which, starts, planes):
        extra = extras(0, which, starts, planes)
        for s in range(width // WB):
            tile = pl.ds(s * WB, WB)
            for z0, first in spans(starts, planes):
                for c in range(planes):
                    z = z0 + c
                    centre = fields[0][which][z + HALO, tile]
                    advance(0, which, z, tile, centre, laps[which, z, tile], extra(z, first + c, s, tile))

    def whole(step, which, starts, planes):
        extra = extras(step, which, starts, planes)

        def use(z, at, s, tile, centre, lap):
            if which == 0:
                see(step, z, s, tile, lap)
            advance(step, which, z, tile, centre, lap, extra(z, at, s, tile))

        laplace(fields[step % 2][which], starts, planes, use)

    def inner(body, first=0, last=(depth - 2 * HALO) // BLOCK):
        def turn(c, _):
            body([pl.multiple_of(c * BLOCK + HALO, CHUNK)], BLOCK)
            return 0

        lax.fori_loop(first, last, turn, 0)

    def pass_on_near(h):
        row_copy(0, h).wait_recv()
        row_copy(1, h).start()
        for dx in (1, 3, 2):
            piece_copy(dx, 1, h).start()

        @pl.when(has_extra)
        def _():
            row_copy(2, h).wait_recv()

        for dx in range(1, COLS):
            first = slab_row(dx)

            @pl.when(first < 0)
            def _():
                piece_copy(dx, -1, h).start()

    def pass_on_later(h):
        row_copy(1, h).wait_recv()
        for dx in (1, 3, 2):

            @pl.when(slab_row(dx) >= 0)
            def _():
                piece_copy(dx, 2, h).start()

    def build_model(h):
        pieces_arrived(h)
        for s in range(WB):
            model[pl.ds(h * half, half), pl.ds(s * WB, WB), :] = pieces[h][offset + SPREAD + s] * (1.0 / SCALE)

    ends = (0, depth - CHUNK)
    for copy in loads[:2]:
        copy.wait()
    inner(functools.partial(first_part, 0))
    row_copy(0, 0).wait_send()
    rows_start(1)
    inner(functools.partial(first_part, 1))
    for h in range(PARTS):
        pass_on_near(h)
    for h in range(PARTS):
        pass_on_later(h)
    for which in range(2):
        for side in range(2):
            halo_start(0, which, side)
    for copy in loads[2:4]:
        copy.wait()
    build_model(0)
    for which in range(2):
        inner(functools.partial(second_part, which), 0, 1)
    for which in range(2):
        for side in range(2):
            halo_arrived(0, which, side)
        first_part(which, ends, CHUNK)
    build_model(1)
    for which in range(2):
        second_part(which, ends, CHUNK)
        for side in range(2):
            halo_start(1, which, side)
    for which in range(2):
        inner(functools.partial(second_part, which), 1)

    def image_out(h):
        place = pl.ds(h * half, half)
        for j in range(SPAN):
            outgoing[j, place] = shown[j + 2 - offset, place]
        for r in (2, -1):
            parts_start(r, h)

    from_row[:, 3] = jnp.zeros((COLS - 1, depth, WB, across), jnp.float32)
    for step in range(1, STEPS):
        for which in range(2):
            body = functools.partial(whole, step, which)
            for side in range(2):
                halo_arrived(step, which, side)
                if step > 1:
                    halo_sent(step - 1, which, side)
            body(ends, CHUNK)
            if step < STEPS - 1:
                for side in range(2):
                    halo_start(step + 1, which, side)
                inner(body)
            elif which == 0:
                inner(body, 0, 1)
                image_out(0)
                inner(body, 1)
                image_out(1)
            else:
                for h in range(PARTS):
                    parts_start(1, h)
                inner(body)
    for h in range(PARTS):
        sum_start(1, h)

        @pl.when(has_extra)
        def _():
            sum_start(2, h)

        @pl.when(col == COLS - 1)
        def _():
            far_part(h).start()

        parts_start(0, h)
    for h in range(PARTS):
        sum_start(0, h)

    @pl.when(col == 1)
    def _():
        from_rows[2] = jnp.zeros((depth, WB, across), jnp.float32)

    for h in range(PARTS):
        parts_arrived(0, h)
        sum_copy(0, h).wait_recv()

        @pl.when(col != 1)
        def _():
            sum_copy(2, h).wait_recv()

        def add_up(place):
            gradient_out[place] = summed(0, True, place) + from_rows[0, place] + from_rows[2, place]

        over_half(h, add_up)
    for which in range(2):
        for side in range(2):
            halo_sent(0, which, side)
            halo_sent(STEPS - 1, which, side)
    for h in range(PARTS):
        if h > 0:
            row_copy(0, h).wait_send()
        row_copy(1, h).wait_send()
        for i in (0, 1):
            sum_copy(i, h).wait_send()

        @pl.when(has_extra)
        def _():
            row_copy(2, h).wait_send()
            sum_copy(2, h).wait_send()

        for dx in range(1, COLS):
            for t in range(3):
                piece_copy(dx, slab_row(dx) + t, h).wait_send()
                part_copy(dx, first_row(col, dx) + t, h).wait_send()


def write_out(*refs):
    copies = [pltpu.make_async_copy(refs[i], refs[3 + i], refs[6].at[i]) for i in range(3)]
    for copy in copies:
        copy.start()
    for copy in copies:
        copy.wait()


def per_device(
    squared_courant,
    window_offset,
    field_last,
    field_after,
    adjoint_last,
    adjoint_after,
    source_place,
    source_wavelet,
    receiver_place,
    receiver_trace,
):
    _, depth, width, across = field_last.shape
    smem = pl.BlockSpec(memory_space=pltpu.SMEM)
    vmem = pl.BlockSpec(memory_space=pltpu.VMEM)
    hbm = pl.BlockSpec(memory_space=pl.ANY)
    f32 = jnp.float32
    dma = pltpu.SemaphoreType.DMA
    field, adjoint, gradient = pl.pallas_call(
        kernel,
        out_shape=(
            pltpu.VMEM((depth, width, across), f32),
            pltpu.VMEM((depth, width, across), f32),
            pltpu.VMEM((depth, WB, across), f32),
        ),
        in_specs=[smem] * 3 + [hbm] * 7,
        out_specs=(vmem, vmem, vmem),
        scratch_shapes=[
            *[pltpu.VMEM((depth + 2 * HALO, width, across), f32)] * 4,
            *[pltpu.VMEM((SPAN + 1, depth // PARTS, WB, across), f32)] * PARTS,
            pltpu.VMEM((2, depth, width, across), f32),
            pltpu.VMEM((depth, width, across), f32),
            pltpu.VMEM((depth, width, across), f32),
            pltpu.VMEM((SPAN + 4, depth, WB, across), f32),
            pltpu.VMEM((SPAN, depth, WB, across), f32),
            pltpu.VMEM((COLS - 1, 4, depth, WB, across), f32),
            pltpu.VMEM((3, depth, WB, across), f32),
            pltpu.VMEM((3, depth, WB, across), f32),
            pltpu.VMEM((3, 1, across), jnp.int32),
            pltpu.VMEM((STEPS, across), f32),
            pltpu.VMEM((width, across), f32),
            pltpu.VMEM((depth * width, across), jnp.bfloat16),
            pltpu.VMEM((STEPS, across, 2 * across), jnp.bfloat16),
            dma((8,)),
            dma((STEPS, 2, 2)),
            dma((STEPS, 2, 2)),
            dma((3, PARTS)),
            dma((3, PARTS)),
            dma((COLS - 1, 3, PARTS)),
            dma((SPAN, PARTS)),
            dma((COLS - 1, 3, PARTS)),
            dma((COLS - 1, 3, PARTS)),
            dma((3, PARTS)),
            dma((3, PARTS)),
        ],
        compiler_params=pltpu.CompilerParams(
            collective_id=0, has_side_effects=True, vmem_limit_bytes=56 * 1024 * 1024
        ),
        name="inversion",
    )(
        window_offset,
        source_place[0],
        source_wavelet[0],
        receiver_place.transpose(1, 0, 2),
        receiver_trace[0],
        squared_courant,
        field_last[0],
        field_after[0],
        adjoint_last[0],
        adjoint_after[0],
    )
    results = pl.pallas_call(
        write_out,
        out_shape=tuple(jax.ShapeDtypeStruct(x.shape, f32) for x in (field, adjoint, gradient)),
        in_specs=[vmem] * 3,
        out_specs=(hbm, hbm, hbm),
        scratch_shapes=[dma((3,))],
        compiler_params=pltpu.CompilerParams(vmem_limit_bytes=4 * 1024 * 1024),
        name="write_out",
    )(field, adjoint, gradient)
    return results[0][None], results[1][None], results[2]


def solution(mesh):
    placed = (
        P("gz", "shot", None),
        P("shot"),
        P("shot", "gz", None, None),
        P("shot", "gz", None, None),
        P("shot", "gz", None, None),
        P("shot", "gz", None, None),
        P("shot", None),
        P("shot", None),
        P("shot", None, None),
        P("shot", None, None),
    )
    return jax.shard_map(
        per_device,
        mesh=mesh,
        in_specs=placed,
        out_specs=(P("shot", "gz", None, None), P("shot", "gz", None, None), P("gz", "shot", None)),
        check_vma=False,
    )
```

```python
import functools
import math

import jax
import jax.numpy as jnp
from jax import lax
from jax.experimental import pallas as pl
from jax.experimental.pallas import tpu as pltpu
from jax.sharding import PartitionSpec as P

WB = 8
COLS = 4
FIRST = (0, 1, -2, -1)
SPREAD = 2
STEPS = 4
SPAN = WB + 2 * SPREAD
FAR = WB + SPREAD - 1
HALO = 4
CHUNK = 4
BLOCK = 12
PARTS = 2
SCALE = 5040.0
CENTRE = -3.0 * 14350.0
SIDE = (8064.0, -1008.0, 128.0, -9.0)
MESH = pl.DeviceIdType.MESH


def banded(rows, cols, period):
    i = lax.broadcasted_iota(jnp.int32, (rows, cols), 0)
    j = lax.broadcasted_iota(jnp.int32, (rows, cols), 1)
    gap = jnp.abs(lax.rem(i, period) - lax.rem(j, period))
    band = jnp.zeros((rows, cols), jnp.float32)
    for k in range(1, 5):
        band = jnp.where(gap == k, SIDE[k - 1], band)
    return band.astype(jnp.bfloat16)


def in_two(values):
    high = values.astype(jnp.bfloat16)
    low = (values - high.astype(jnp.float32)).astype(jnp.bfloat16)
    return high, low


def kernel(
    offset_ref,
    spot_ref,
    wavelet_ref,
    receivers_in,
    traces_in,
    courant_ref,
    field_last,
    field_after,
    adjoint_last,
    adjoint_after,
    field_out,
    adjoint_out,
    gradient_out,
    field_a,
    adjoint_a,
    field_b,
    adjoint_b,
    pieces_low,
    pieces_high,
    laps,
    model,
    imaging,
    shown,
    outgoing,
    from_row,
    sums,
    from_rows,
    receivers_ref,
    traces_ref,
    taper_ref,
    hits,
    amounts,
    load_sem,
    halo_send,
    halo_recv,
    row_send,
    row_recv,
    far_send,
    far_recv,
    relay_send,
    relay_recv,
    piece_send,
    piece_recv,
    back_send,
    back_recv,
    sum_send,
    sum_recv,
):
    fields = ((field_a, adjoint_a), (field_b, adjoint_b))
    pieces = (pieces_low, pieces_high)
    shot = lax.axis_index("shot")
    slab = lax.axis_index("gz")
    shots = lax.axis_size("shot")
    slabs = lax.axis_size("gz")
    depth, width, across = field_last.shape
    chunks = depth // CHUNK
    half = depth // PARTS
    quarter = half // 2
    stretches = ((0, 0, 0, quarter), (0, depth - quarter, quarter, quarter), (1, quarter, 0, half))
    has = (slab > 0, slab < slabs - 1)
    beside = (jnp.maximum(slab - 1, 0), jnp.minimum(slab + 1, slabs - 1))

    row, col = shot // COLS, lax.rem(shot, COLS)
    rows = shots // COLS
    has_extra = col > 1
    is_far = (col == 0) | (col == COLS - 1)
    far_shot = lax.rem(jnp.where(col == 0, shot - FAR, shot + FAR) + shots, shots)

    def in_row(dx):
        return row * COLS + lax.rem(col + dx, COLS)

    def in_column(r):
        return lax.rem(row + r + rows, rows) * COLS + col

    def first_row(source, dx):
        return (source + FIRST[dx] - lax.rem(source + dx, COLS)) // COLS

    loads = []
    for i, (buffer, which, source) in enumerate(
        ((0, 0, field_last), (0, 1, adjoint_last), (1, 0, field_after), (1, 1, adjoint_after))
    ):
        loads.append(pltpu.make_async_copy(source, fields[buffer][which].at[pl.ds(HALO, depth)], load_sem.at[i]))
    for i, (source, place) in enumerate(
        (
            *(
                (courant_ref.at[pl.ds(plane, count)], pieces[h].at[SPREAD, pl.ds(at, count)])
                for h, plane, at, count in stretches
            ),
            (receivers_in, receivers_ref),
            (traces_in, traces_ref),
        )
    ):
        loads.append(pltpu.make_async_copy(source, place, load_sem.at[4 + i]))
    for copy in loads:
        copy.start()

    blank = jnp.zeros((HALO, width, across), jnp.float32)
    for side, place in ((0, 0), (1, HALO + depth)):

        @pl.when(jnp.logical_not(has[side]))
        def _():
            for buffer in range(2):
                for which in range(2):
                    fields[buffer][which][pl.ds(place, HALO)] = blank

    barrier = pltpu.get_barrier_semaphore()
    for dx in range(1, COLS):
        pl.semaphore_signal(barrier, inc=1, device_id={"shot": in_row(dx)}, device_id_type=MESH)
    for r in (-1, 1):
        pl.semaphore_signal(barrier, inc=1, device_id={"shot": in_column(r)}, device_id_type=MESH)

    @pl.when(is_far)
    def _():
        pl.semaphore_signal(barrier, inc=1, device_id={"shot": far_shot}, device_id_type=MESH)

    for side in range(2):

        @pl.when(has[side])
        def _():
            pl.semaphore_signal(barrier, inc=1, device_id={"gz": beside[side]}, device_id_type=MESH)

    beside_count = jnp.where(has[0], 1, 0) + jnp.where(has[1], 1, 0)
    pl.semaphore_wait(barrier, COLS - 1 + 2 + jnp.where(is_far, 1, 0) + beside_count)

    def halo(turn, which, side):
        place = HALO if side == 0 else depth
        landing = HALO + depth if side == 0 else 0
        if turn == 0:
            source = (field_last, adjoint_last)[which].at[pl.ds(place - HALO, HALO)]
        else:
            source = fields[turn % 2][which].at[pl.ds(place, HALO)]
        return pltpu.make_async_remote_copy(
            src_ref=source,
            dst_ref=fields[turn % 2][which].at[pl.ds(landing, HALO)],
            send_sem=halo_send.at[turn, which, side],
            recv_sem=halo_recv.at[turn, which, side],
            device_id={"gz": beside[side]},
            device_id_type=MESH,
        )

    def halo_start(turn, which, side):
        @pl.when(has[side])
        def _():
            halo(turn, which, side).start()

    def halo_arrived(turn, which, side):
        @pl.when(has[side])
        def _():
            halo(turn, which, 1 - side).wait_recv()

    def halo_sent(turn, which, side):
        @pl.when(has[side])
        def _():
            halo(turn, which, side).wait_send()

    def own_copy(t, slot, send, recv, target):
        h, plane, at, count = stretches[t]
        return pltpu.make_async_remote_copy(
            src_ref=courant_ref.at[pl.ds(plane, count)],
            dst_ref=pieces[h].at[slot, pl.ds(at, count)],
            send_sem=send,
            recv_sem=recv,
            device_id={"shot": target},
            device_id_type=MESH,
        )

    def near_copy(i, t):
        slot = (SPREAD + COLS, SPAN)[i]
        return own_copy(t, slot, row_send.at[i, t], row_recv.at[i, t], in_column((-1, 1)[i]))

    def far_copy(t):
        return own_copy(t, SPAN - 1, far_send.at[t], far_recv.at[t], far_shot)

    def in_part(h):
        return [t for t in range(len(stretches)) if stretches[t][0] == h]

    def relay_copy(h):
        return pltpu.make_async_remote_copy(
            src_ref=pieces[h].at[SPREAD + COLS],
            dst_ref=pieces[h].at[SPREAD + 2 * COLS],
            send_sem=relay_send.at[h],
            recv_sem=relay_recv.at[h],
            device_id={"shot": in_column(-1)},
            device_id_type=MESH,
        )

    def piece_copy(dx, r, h):
        target = lax.rem(col + dx, COLS)
        slot = COLS * r + col - target + SPREAD
        held = jnp.where(r >= 0, jnp.minimum(SPREAD + COLS * r, SPAN), SPAN)
        return pltpu.make_async_remote_copy(
            src_ref=pieces[h].at[held],
            dst_ref=pieces[h].at[slot],
            send_sem=piece_send.at[dx - 1, r - slab_row(dx), h],
            recv_sem=piece_recv.at[slot, h],
            device_id={"shot": in_row(dx)},
            device_id_type=MESH,
        )

    def far_part(h):
        return pltpu.make_async_remote_copy(
            src_ref=outgoing.at[SPAN - 1, pl.ds(h * half, half)],
            dst_ref=from_rows.at[2, pl.ds(h * half, half)],
            send_sem=back_send.at[0, 2, h],
            recv_sem=sum_recv.at[2, h],
            device_id={"shot": far_shot},
            device_id_type=MESH,
        )

    def slab_row(dx):
        return first_row(lax.rem(col + dx, COLS), COLS - dx)

    def pieces_arrived(h):
        for j in range(SPAN - 1):
            if j % COLS != SPREAD:
                pltpu.make_async_copy(pieces[h].at[j], pieces[h].at[j], piece_recv.at[j, h]).wait()

        @pl.when(col == COLS - 1)
        def _():
            for t in in_part(h):
                far_copy(t).wait_recv()

        @pl.when(col != COLS - 1)
        def _():
            j = SPAN - 1
            pltpu.make_async_copy(pieces[h].at[j], pieces[h].at[j], piece_recv.at[j, h]).wait()

    def part_copy(dx, r, h):
        target = lax.rem(col + dx, COLS)
        at = r - first_row(col, dx)
        return pltpu.make_async_remote_copy(
            src_ref=outgoing.at[COLS * r + target - col + SPREAD, pl.ds(h * half, half)],
            dst_ref=from_row.at[dx - 1, at, pl.ds(h * half, half)],
            send_sem=back_send.at[dx - 1, at, h],
            recv_sem=back_recv.at[dx - 1, at, h],
            device_id={"shot": in_row(dx)},
            device_id_type=MESH,
        )

    def parts_start(r, h):
        for dx in (1, 3, 2):
            first = first_row(col, dx)

            @pl.when((r >= first) & (r <= first + 2))
            def _():
                part_copy(dx, r, h).start()

    def source_row(dx):
        return first_row(lax.rem(col - dx + COLS, COLS), dx)

    def parts_arrived(r, h):
        for dx in range(1, COLS):
            first = source_row(dx)

            @pl.when((r >= first) & (r <= first + 2))
            def _():
                place = from_row.at[dx - 1, r - first, pl.ds(h * half, half)]
                pltpu.make_async_copy(place, place, back_recv.at[dx - 1, r - first, h]).wait()

    def summed(r, own, place):
        total = outgoing[SPREAD + COLS * r, place] if own else jnp.zeros((CHUNK, WB, across), jnp.float32)
        for dx in range(1, COLS):
            at = r - source_row(dx)
            total = total + from_row[dx - 1, jnp.where((at >= 0) & (at <= 2), at, 3), place]
        return total

    def sum_copy(i, h):
        return pltpu.make_async_remote_copy(
            src_ref=sums.at[i, pl.ds(h * half, half)],
            dst_ref=from_rows.at[i, pl.ds(h * half, half)],
            send_sem=sum_send.at[i, h],
            recv_sem=sum_recv.at[i, h],
            device_id={"shot": in_column((1, 1, -1)[i])},
            device_id_type=MESH,
        )

    def over_half(h, body):
        def turn(c, _):
            body(pl.ds(pl.multiple_of(c * CHUNK, CHUNK), CHUNK))
            return 0

        count = half // CHUNK
        lax.fori_loop(h * count, (h + 1) * count, turn, 0)

    def sum_start(i, h):
        r = (1, 2, -1)[i]
        parts_arrived(r, h)
        if i == 0:
            sum_copy(1, h).wait_recv()

        def body(place):
            total = summed(r, i < 2, place)
            sums[i, place] = total + from_rows[1, place] if i == 0 else total

        over_half(h, body)
        sum_copy(i, h).start()

    def rows_start(h):
        for t in in_part(h):
            near_copy(0, t).start()

        @pl.when(has_extra)
        def _():
            for t in in_part(h):
                near_copy(1, t).start()

    rows_start(0)
    for h in range(PARTS):
        for t in in_part(h):
            loads[4 + t].wait()
        for dx in (1, 3, 2):

            @pl.when(slab_row(dx) <= 0)
            def _():
                piece_copy(dx, 0, h).start()

        @pl.when(col == 0)
        def _():
            for t in in_part(h):
                far_copy(t).start()

    offset = offset_ref[0]
    for copy in loads[7:]:
        copy.wait()
    by_y = banded(2 * across, across, across)
    by_x = banded(width, 2 * width, width)
    cell = lax.broadcasted_iota(jnp.int32, (width * CHUNK, across), 0)
    place = (receivers_ref[0] - slab * depth) * width + receivers_ref[1]

    def mark(c, _):
        start = pl.multiple_of(c * CHUNK * width, CHUNK * width)
        hits[pl.ds(start, CHUNK * width), :] = jnp.where(cell + start == place, 1.0, 0.0).astype(jnp.bfloat16)
        return 0

    lax.fori_loop(0, chunks, mark, 0)
    along = lax.broadcasted_iota(jnp.int32, (across, across), 0) == receivers_ref[2]
    for step in range(STEPS):
        high, low = in_two(jnp.where(along, traces_ref[step : step + 1, :], 0.0))
        amounts[step, :, 0:across] = high
        amounts[step, :, across : 2 * across] = low
    across_x = lax.broadcasted_iota(jnp.int32, (width, across), 0).astype(jnp.float32)
    taper_ref[...] = jnp.sin((across_x + 0.5) * (math.pi / width)) ** 2 * (1.0 / SCALE)
    spot = jnp.where(
        (lax.broadcasted_iota(jnp.int32, (width, across), 0) == spot_ref[1])
        & (lax.broadcasted_iota(jnp.int32, (width, across), 1) == spot_ref[2]),
        1.0,
        0.0,
    )
    spot_depth = spot_ref[0] - slab * depth
    shown[pl.ds(0, 4)] = jnp.zeros((4, depth, WB, across), jnp.float32)
    shown[pl.ds(12, 4)] = jnp.zeros((4, depth, WB, across), jnp.float32)

    def flat(high, low, planes):
        rows = planes * width
        left = jnp.concatenate([high.reshape(rows, across), low.reshape(rows, across)], axis=1)
        in_y = jnp.dot(left, by_y, preferred_element_type=jnp.float32)
        right = jnp.concatenate(
            [jnp.concatenate([part[c] for c in range(planes)], axis=1) for part in (high, low)], axis=0
        )
        in_x = jnp.dot(by_x, right, preferred_element_type=jnp.float32)
        return in_y, in_x

    def spans(starts, planes):
        return [(z0, i * planes) for i, z0 in enumerate(starts)]

    def injected(step, starts, planes):
        found = []
        for z0 in starts:
            found.append(hits[pl.ds(pl.multiple_of(z0 * width, CHUNK * width), planes * width), :])
        found = jnp.concatenate(found, axis=0)
        return lax.dot_general(
            jnp.concatenate([found, found], axis=1),
            amounts[step],
            (((1,), (1,)), ((), ())),
            preferred_element_type=jnp.float32,
        )

    def laplace(now, starts, planes, use):
        high, low = in_two(jnp.concatenate([now[pl.ds(z0 + HALO, planes)] for z0 in starts], axis=0))
        in_y, in_x = flat(high, low, planes * len(starts))
        for s in range(width // WB):
            tile = pl.ds(s * WB, WB)
            for z0, first in spans(starts, planes):
                line = [now[z0 + c, tile] for c in range(planes + 2 * HALO)]
                for c in range(planes):
                    at = first + c
                    centre = line[c + HALO]
                    total = CENTRE * centre + in_y[at * width + s * WB : at * width + (s + 1) * WB]
                    total = total + in_x[s * WB : (s + 1) * WB, at * across : (at + 1) * across]
                    for k in range(1, 5):
                        total = total + SIDE[k - 1] * (line[c + HALO + k] + line[c + HALO - k])
                    use(z0 + c, at, s, tile, centre, total)

    def see(step, z, s, tile, lap):
        seen = fields[step % 2][1][z + HALO, tile] * lap
        if step > 0:
            seen = imaging[z, tile] + seen
        if step < STEPS - 1:
            imaging[z, tile] = seen
        else:
            shown[4 + s, z] = taper_ref[tile] * seen

    def advance(step, which, z, tile, centre, lap, extra):
        later = fields[1 - step % 2][which]
        new = 2.0 * centre - later[z + HALO, tile] + model[z, tile] * lap + extra
        if step < STEPS - 1:
            later[z + HALO, tile] = new
        else:
            (field_out, adjoint_out)[which][z, tile] = new

    def extras(step, which, starts, planes):
        if which == 0:
            return lambda z, at, s, tile: spot[s * WB : (s + 1) * WB] * jnp.where(
                z == spot_depth, wavelet_ref[step], 0.0
            )
        added = injected(step, starts, planes)
        return lambda z, at, s, tile: added[at * width + s * WB : at * width + (s + 1) * WB]

    def first_part(which, starts, planes):
        def use(z, at, s, tile, centre, lap):
            laps[which, z, tile] = lap
            if which == 0:
                see(0, z, s, tile, lap)

        laplace(fields[0][which], starts, planes, use)

    def second_part(which, starts, planes):
        extra = extras(0, which, starts, planes)
        for s in range(width // WB):
            tile = pl.ds(s * WB, WB)
            for z0, first in spans(starts, planes):
                for c in range(planes):
                    z = z0 + c
                    centre = fields[0][which][z + HALO, tile]
                    advance(0, which, z, tile, centre, laps[which, z, tile], extra(z, first + c, s, tile))

    def whole(step, which, starts, planes):
        extra = extras(step, which, starts, planes)

        def use(z, at, s, tile, centre, lap):
            if which == 0:
                see(step, z, s, tile, lap)
            advance(step, which, z, tile, centre, lap, extra(z, at, s, tile))

        laplace(fields[step % 2][which], starts, planes, use)

    def inner(body, first=0, last=(depth - 2 * HALO) // BLOCK):
        def turn(c, _):
            body([pl.multiple_of(c * BLOCK + HALO, CHUNK)], BLOCK)
            return 0

        lax.fori_loop(first, last, turn, 0)

    def pass_on_near(h):
        for t in in_part(h):
            near_copy(0, t).wait_recv()
        relay_copy(h).start()
        for dx in (1, 3, 2):
            piece_copy(dx, 1, h).start()

        @pl.when(has_extra)
        def _():
            for t in in_part(h):
                near_copy(1, t).wait_recv()

        for dx in range(1, COLS):

            @pl.when(slab_row(dx) < 0)
            def _():
                piece_copy(dx, -1, h).start()

    def pass_on_later(h):
        relay_copy(h).wait_recv()
        for dx in (1, 3, 2):

            @pl.when(slab_row(dx) >= 0)
            def _():
                piece_copy(dx, 2, h).start()

    def build_model(h):
        pieces_arrived(h)
        for t in in_part(h):
            _, plane, at, count = stretches[t]
            for s in range(WB):
                found = pieces[h][offset + SPREAD + s, pl.ds(at, count)]
                model[pl.ds(plane, count), pl.ds(s * WB, WB), :] = found * (1.0 / SCALE)

    def first_ends(which):
        for side in range(2):
            halo_arrived(0, which, side)
        first_part(which, ends, CHUNK)

    ends = (0, depth - CHUNK)
    for copy in loads[:2]:
        copy.wait()
    inner(functools.partial(first_part, 0))
    for t in in_part(0):
        near_copy(0, t).wait_send()
    rows_start(1)
    for side in range(2):
        halo_start(0, 0, side)
    inner(functools.partial(first_part, 1))
    for h in range(PARTS):
        pass_on_near(h)
    first_ends(0)
    for h in range(PARTS):
        pass_on_later(h)
    for side in range(2):
        halo_start(0, 1, side)
    for copy in loads[2:4]:
        copy.wait()
    build_model(0)
    for which in range(2):
        if which == 1:
            first_ends(1)
        second_part(which, ends, CHUNK)
        for side in range(2):
            halo_start(1, which, side)
    build_model(1)
    for which in range(2):
        inner(functools.partial(second_part, which))

    def image_out(h):
        place = pl.ds(h * half, half)
        for j in range(SPAN):
            outgoing[j, place] = shown[j + 2 - offset, place]
        for r in (2, -1):
            parts_start(r, h)

    from_row[:, 3] = jnp.zeros((COLS - 1, depth, WB, across), jnp.float32)
    for step in range(1, STEPS):
        for which in range(2):
            body = functools.partial(whole, step, which)
            for side in range(2):
                halo_arrived(step, which, side)
                if step > 1:
                    halo_sent(step - 1, which, side)
            body(ends, CHUNK)
            if step < STEPS - 1:
                for side in range(2):
                    halo_start(step + 1, which, side)
                inner(body)
            elif which == 0:
                inner(body, 0, 1)
                image_out(0)
                inner(body, 1)
                image_out(1)
            else:
                inner(body)
    def last_wave():
        for h in range(PARTS):
            parts_start(0, h)

            @pl.when(col == COLS - 1)
            def _():
                far_part(h).start()

    for h in range(PARTS):
        sum_start(1, h)
        parts_start(1, h)

        @pl.when(has_extra)
        def _():
            sum_start(2, h)

    sum_start(0, 0)
    last_wave()
    sum_start(0, 1)

    @pl.when(col == 1)
    def _():
        from_rows[2] = jnp.zeros((depth, WB, across), jnp.float32)

    for h in range(PARTS):
        parts_arrived(0, h)
        sum_copy(0, h).wait_recv()

        @pl.when(col != 1)
        def _():
            sum_copy(2, h).wait_recv()

        def add_up(place):
            gradient_out[place] = summed(0, True, place) + from_rows[0, place] + from_rows[2, place]

        over_half(h, add_up)
    for which in range(2):
        for side in range(2):
            halo_sent(0, which, side)
            halo_sent(STEPS - 1, which, side)
    for t in range(len(stretches)):
        if t not in in_part(0):
            near_copy(0, t).wait_send()

        @pl.when(has_extra)
        def _():
            near_copy(1, t).wait_send()

        @pl.when(col == 0)
        def _():
            far_copy(t).wait_send()

    for h in range(PARTS):
        relay_copy(h).wait_send()
        for i in (0, 1):
            sum_copy(i, h).wait_send()

        @pl.when(has_extra)
        def _():
            sum_copy(2, h).wait_send()

        for dx in range(1, COLS):
            for t in range(3):

                @pl.when(slab_row(dx) + t < 3)
                def _():
                    piece_copy(dx, slab_row(dx) + t, h).wait_send()

                part_copy(dx, first_row(col, dx) + t, h).wait_send()


def write_out(*refs):
    copies = [pltpu.make_async_copy(refs[i], refs[3 + i], refs[6].at[i]) for i in range(3)]
    for copy in copies:
        copy.start()
    for copy in copies:
        copy.wait()


def per_device(
    squared_courant,
    window_offset,
    field_last,
    field_after,
    adjoint_last,
    adjoint_after,
    source_place,
    source_wavelet,
    receiver_place,
    receiver_trace,
):
    _, depth, width, across = field_last.shape
    smem = pl.BlockSpec(memory_space=pltpu.SMEM)
    vmem = pl.BlockSpec(memory_space=pltpu.VMEM)
    hbm = pl.BlockSpec(memory_space=pl.ANY)
    f32 = jnp.float32
    dma = pltpu.SemaphoreType.DMA
    field, adjoint, gradient = pl.pallas_call(
        kernel,
        out_shape=(
            pltpu.VMEM((depth, width, across), f32),
            pltpu.VMEM((depth, width, across), f32),
            pltpu.VMEM((depth, WB, across), f32),
        ),
        in_specs=[smem] * 3 + [hbm] * 7,
        out_specs=(vmem, vmem, vmem),
        scratch_shapes=[
            *[pltpu.VMEM((depth + 2 * HALO, width, across), f32)] * 4,
            *[pltpu.VMEM((SPAN + 1, depth // PARTS, WB, across), f32)] * PARTS,
            pltpu.VMEM((2, depth, width, across), f32),
            pltpu.VMEM((depth, width, across), f32),
            pltpu.VMEM((depth, width, across), f32),
            pltpu.VMEM((SPAN + 4, depth, WB, across), f32),
            pltpu.VMEM((SPAN, depth, WB, across), f32),
            pltpu.VMEM((COLS - 1, 4, depth, WB, across), f32),
            pltpu.VMEM((3, depth, WB, across), f32),
            pltpu.VMEM((3, depth, WB, across), f32),
            pltpu.VMEM((3, 1, across), jnp.int32),
            pltpu.VMEM((STEPS, across), f32),
            pltpu.VMEM((width, across), f32),
            pltpu.VMEM((depth * width, across), jnp.bfloat16),
            pltpu.VMEM((STEPS, across, 2 * across), jnp.bfloat16),
            dma((9,)),
            dma((STEPS, 2, 2)),
            dma((STEPS, 2, 2)),
            dma((2, 3)),
            dma((2, 3)),
            dma((3,)),
            dma((3,)),
            dma((PARTS,)),
            dma((PARTS,)),
            dma((COLS - 1, 3, PARTS)),
            dma((SPAN, PARTS)),
            dma((COLS - 1, 3, PARTS)),
            dma((COLS - 1, 3, PARTS)),
            dma((3, PARTS)),
            dma((3, PARTS)),
        ],
        compiler_params=pltpu.CompilerParams(
            collective_id=0, has_side_effects=True, vmem_limit_bytes=56 * 1024 * 1024
        ),
        name="inversion",
    )(
        window_offset,
        source_place[0],
        source_wavelet[0],
        receiver_place.transpose(1, 0, 2),
        receiver_trace[0],
        squared_courant,
        field_last[0],
        field_after[0],
        adjoint_last[0],
        adjoint_after[0],
    )
    results = pl.pallas_call(
        write_out,
        out_shape=tuple(jax.ShapeDtypeStruct(x.shape, f32) for x in (field, adjoint, gradient)),
        in_specs=[vmem] * 3,
        out_specs=(hbm, hbm, hbm),
        scratch_shapes=[dma((3,))],
        compiler_params=pltpu.CompilerParams(vmem_limit_bytes=4 * 1024 * 1024),
        name="write_out",
    )(field, adjoint, gradient)
    return results[0][None], results[1][None], results[2]


def solution(mesh):
    placed = (
        P("gz", "shot", None),
        P("shot"),
        P("shot", "gz", None, None),
        P("shot", "gz", None, None),
        P("shot", "gz", None, None),
        P("shot", "gz", None, None),
        P("shot", None),
        P("shot", None),
        P("shot", None, None),
        P("shot", None, None),
    )
    return jax.shard_map(
        per_device,
        mesh=mesh,
        in_specs=placed,
        out_specs=(P("shot", "gz", None, None), P("shot", "gz", None, None), P("gz", "shot", None)),
        check_vma=False,
    )
```
